32 devices in a mesh: groups: 2 (over y), expert: 8 (over z, x), tensor: 2 (over core).
Axes of the slice: x: 2, y: 2, z: 4, core: 2. Of those that a mesh axis runs over, the one named last changes fastest.
Arguments:
- tokens: bfloat16 [2048, 4096], P(('groups', 'expert'), 'tensor'), parts along dimension 0, may hold values from -6 to 6
- grad_query: bfloat16 [2048, 4096], P(('groups', 'expert'), 'tensor'), parts along dimension 0, may hold values from -0.29882812 to 0.29882812
- grad_value: bfloat16 [2048, 1024], P(('groups', 'expert'), 'tensor'), parts along dimension 0, may hold values from -0.29882812 to 0.29882812
- a_proj: bfloat16 [16, 4096, 128], P(('groups', 'expert'), 'tensor'), parts along dimension 0, may hold values from -0.09375 to 0.09375
- b_query: bfloat16 [16, 64, 4096], P(('groups', 'expert'), None, 'tensor'), parts along dimension 0, may hold values from -0.75 to 0.75
- b_value: bfloat16 [16, 64, 1024], P(('groups', 'expert'), None, 'tensor'), parts along dimension 0, may hold values from -0.75 to 0.75
- token_request: int32 [16, 128], P(('groups', 'expert')), parts along dimension 0, may hold values from 0 to 31, never falling along the last dimension, each value on 1 to 5 neighbouring positions
- req_adapter: int32 [16, 32, 4], P(('groups', 'expert')), parts along dimension 0, may hold values from 0 to 7, as said below
- req_count: int32 [16, 32], P(('groups', 'expert')), parts along dimension 0, may hold values from 1 to 4
- req_mix: bfloat16 [16, 32, 4], P(('groups', 'expert')), parts along dimension 0, may hold values from 0.19921875 to 1.5
Outputs:
- out_query: bfloat16 [2048, 4096], P(('groups', 'expert'), 'tensor'), parts along dimension 0
- out_value: bfloat16 [2048, 1024], P(('groups', 'expert'), 'tensor'), parts along dimension 0
- grad_a: bfloat16 [16, 4096, 128], P(('groups', 'expert'), 'tensor'), parts along dimension 0
- grad_bq: bfloat16 [16, 64, 4096], P(('groups', 'expert'), None, 'tensor'), parts along dimension 0
- grad_bv: bfloat16 [16, 64, 1024], P(('groups', 'expert'), None, 'tensor'), parts along dimension 0
- grad_mix: float32 [16, 32, 4], P(('groups', 'expert')), parts along dimension 0
The draws below stay inside these ranges and needn't reach their ends.
There are 2 independent parts, one for each index of `groups`. The reference program is written for one: setup_inputs(seed, part) draws one part's arguments, and reference() takes and returns one part's arrays. A program takes and returns all parts, laid end to end along the dimension named above; each array names one. Nothing has to cross between parts.
Inputs may be any that keep to these rules, and one draw needn't show every extreme that they name: `req_adapter`: adapter a is held at index a of expert. In each block's 4 * 32 entries (used or not), every adapter appears exactly 4 * 32 / 8 times. `token_request`: never falls along a block; request r of a block holds 1 to 5 tokens, and one request of every block holds exactly 5.
All inputs are finite; a program needn't handle non-finite values.
Results may differ from the reference program's by a relative error of at most 0.0085.
Values may be sent and summed in bfloat16 or wider, within the bound.
No kernel may reach another device: no remote copies, remote signals or barrier semaphores. Data moves between devices by JAX's collectives and lax.ppermute only.
A program may use at most 128 MiB of HBM per device.

```python
import math
import jax
import jax.numpy as jnp
import numpy as np
from jax import lax

D = 4096
DKV = 1024
RANK = 64
REQ_MOST = 5
TOK_DEV = 128
REQ_DEV = 32
ADAPTERS = 8
TOKENS = 1024
N_EXPERT = 8


def draw_req_adapter(key, part):
    key = jax.random.fold_in(key, 7)
    slot_count = 4 * REQ_DEV
    block_keys = jax.random.split(key, N_EXPERT)
    shuffled = jax.vmap(lambda one_key: jax.random.permutation(one_key, slot_count))(block_keys)
    owners = shuffled % N_EXPERT
    return owners.reshape(N_EXPERT, REQ_DEV, 4).astype(jnp.int32)


def place_ends(drawn, key, low, largest):
    place = [jax.random.randint(jax.random.fold_in(key, axis), (), 0, length) for axis, length in enumerate(drawn.shape)]
    main_axis = drawn.shape.index(max(drawn.shape))
    beside = place[:main_axis] + [(place[main_axis] + 1) % drawn.shape[main_axis]] + place[main_axis + 1:]
    return drawn.at[tuple(place)].set(low).at[tuple(beside)].set(largest)


def block_scale(own_key, dims, cuts, low, top_value):
    loudness, own = 1.0, jax.random.fold_in(own_key, 6)
    for position, blocks in cuts:
        draws = jnp.exp(jax.random.uniform(jax.random.fold_in(own, position), (blocks,), jnp.float32, low / len(cuts), top_value / len(cuts)))
        loudness = loudness * jnp.repeat(draws, dims[position] // blocks).reshape([-1 if axis == position else 1 for axis in range(len(dims))])
    return loudness


def profile(amount, total, limit, skew):
    loads = [(1 << 20) // math.isqrt(grade ** skew) + 1 for grade in range(2, amount + 1)]
    surplus, counts = total - limit - (amount - 1), [1] * (amount - 1)
    while surplus > 0:
        candidates = [i for i in range(amount - 1) if counts[i] < limit]
        pool, budget = sum([loads[i] for i in candidates]), surplus
        for i in candidates:
            extra = min(limit - counts[i], max(1, budget * loads[i] // pool), surplus)
            counts[i] = counts[i] + extra
            surplus = surplus - extra
    return np.array([limit] + counts)


def uneven(stream_key, amount, total, most, skew):
    if amount == 2:
        one = jax.random.randint(stream_key, (), max(1, total - most), min(most, total - 1) + 1)
        return jnp.stack([one, total - one])
    sizes = jnp.asarray(profile(amount, total, most, skew), jnp.int32)
    pairs = (amount - 1) // 2
    source_of, sink = sizes[1:1 + 2 * pairs:2], sizes[2:2 + 2 * pairs:2]
    margin = jnp.minimum(source_of - 1, most - sink)
    shifted = jax.random.randint(jax.random.fold_in(stream_key, 1), (pairs,), 0, 1 << 20) % (margin + 1)
    sizes = sizes.at[1:1 + 2 * pairs:2].set(source_of - shifted).at[2:2 + 2 * pairs:2].set(sink + shifted)
    return sizes[jax.random.permutation(jax.random.fold_in(stream_key, 2), amount)]


def noise(stream_key, shape, width, limit, cuts=(), kind=jnp.bfloat16):
    gain = block_scale(stream_key, shape, cuts, -0.22, 0.18) if cuts else 1.0
    entries = jax.random.normal(stream_key, shape, jnp.float32) * width * gain
    return jnp.minimum(jnp.maximum(entries, -limit), limit).astype(kind)


def setup_inputs(seed: int = 0, part: int = 0) -> dict:
    key_of = jax.random.split(jax.random.key(seed), 11)
    part_splits = jax.random.split(jax.random.fold_in(key_of[10], part), 11)
    return {
        "tokens": noise(part_splits[0], (TOKENS, D), 1.0, 6.0, ((0, 8), (1, 2))),
        "grad_query": noise(part_splits[1], (TOKENS, D), 0.05, 0.29882812, ((0, 8), (1, 2))),
        "grad_value": noise(part_splits[2], (TOKENS, DKV), 0.05, 0.29882812, ((0, 8), (1, 2))),
        "a_proj": noise(part_splits[3], (ADAPTERS, D, 2 * RANK), D ** -0.5, 0.09375, ((0, 8), (1, 2))),
        "b_query": noise(part_splits[4], (ADAPTERS, RANK, D), RANK ** -0.5, 0.75, ((0, 8), (2, 2))),
        "b_value": noise(part_splits[5], (ADAPTERS, RANK, DKV), RANK ** -0.5, 0.75, ((0, 8), (2, 2))),
        "token_request": jax.vmap(lambda own: jnp.searchsorted(jnp.cumsum(uneven(own, REQ_DEV, TOK_DEV, REQ_MOST, 1)), jnp.arange(TOK_DEV), side="right"))(jax.random.split(part_splits[6], N_EXPERT)).reshape((N_EXPERT, TOK_DEV)).astype(jnp.int32),
        "req_adapter": draw_req_adapter(jax.random.fold_in(jax.random.fold_in(key_of[10], part), 71), part),
        "req_count": place_ends(jax.random.randint(part_splits[8], (N_EXPERT, REQ_DEV), 1, 5), jax.random.fold_in(part_splits[8], 1), 1, 4).astype(jnp.int32),
        "req_mix": jnp.clip(0.19921875 + 1.3007812 * jax.random.uniform(part_splits[9], (N_EXPERT, REQ_DEV, 4), jnp.float32) ** block_scale(part_splits[9], (N_EXPERT, REQ_DEV, 4), ((0, 8),), -0.2, 0.2), 0.19921875, 1.5).astype(jnp.bfloat16),
    }


def reference(tokens, grad_query, grad_value, a_proj, b_query, b_value, token_request, req_adapter, req_count, req_mix):
    block_count = token_request.shape[0]
    tok_dev = token_request.shape[1]
    requests = req_count.shape[1]
    slot_count = 4 * requests
    row_count = REQ_MOST
    rank_width = a_proj.shape[2] // 2
    adapter_count = a_proj.shape[0]
    per_adapter = block_count * slot_count // adapter_count
    req_ids = jnp.arange(requests, dtype=jnp.int32)
    lengths = jnp.sum((token_request[:, :, None] == req_ids[None, None, :]).astype(jnp.int32), axis=1)
    starts = jnp.cumsum(lengths, axis=1).astype(jnp.int32) - lengths
    owners = req_adapter.reshape(-1)
    slot_order = jnp.argsort(owners, stable=True).astype(jnp.int32).reshape(adapter_count, per_adapter)
    block_of = slot_order // slot_count
    slot_of = slot_order % slot_count
    req_of = slot_of // 4
    pick_of = slot_of % 4
    row_ids = jnp.arange(row_count, dtype=jnp.int32)
    live_rows = (row_ids[None, None, :] < lengths[block_of, req_of][..., None]) & (pick_of < req_count[block_of, req_of])[..., None]
    local_idx = jnp.where(live_rows, starts[block_of, req_of][..., None] + row_ids[None, None, :], 0)
    token_idx = (block_of[..., None] * tok_dev + local_idx).astype(jnp.int32)
    mixing = jnp.where(live_rows, req_mix[block_of, req_of, pick_of][..., None], jnp.zeros((), req_mix.dtype))

    def adapter_step(carried, item_parts):
        sum_query, sum_value, sum_mix = carried
        index_rows, alive_rows, weight_rows, a_matrix, bq_matrix, bv_matrix, slot_flat = item_parts
        flat_rows = index_rows.reshape(-1)
        keep_rows = alive_rows.reshape(-1, 1)
        nothing = jnp.zeros((), tokens.dtype)
        x_rows = jnp.where(keep_rows, tokens[flat_rows], nothing)
        query_rows = jnp.where(keep_rows, grad_query[flat_rows], nothing)
        value_rows = jnp.where(keep_rows, grad_value[flat_rows], nothing)
        hidden = jnp.dot(x_rows, a_matrix, preferred_element_type=jnp.float32)
        slope_query = jnp.dot(query_rows, bq_matrix.T, preferred_element_type=jnp.float32)
        slope_value = jnp.dot(value_rows, bv_matrix.T, preferred_element_type=jnp.float32)
        slopes = jnp.concatenate([slope_query, slope_value], axis=1)
        hidden_bf = hidden.astype(jnp.bfloat16)
        up_query = jnp.dot(hidden_bf[:, :rank_width], bq_matrix, preferred_element_type=jnp.float32).astype(jnp.bfloat16)
        up_value = jnp.dot(hidden_bf[:, rank_width:], bv_matrix, preferred_element_type=jnp.float32).astype(jnp.bfloat16)
        weight_col = weight_rows.reshape(-1, 1).astype(jnp.float32)
        sum_query = sum_query.at[flat_rows].add(weight_col * up_query.astype(jnp.float32))
        sum_value = sum_value.at[flat_rows].add(weight_col * up_value.astype(jnp.float32))
        row_grad = jnp.sum(slopes * hidden_bf.astype(jnp.float32), axis=1).astype(jnp.bfloat16)
        slot_grad = jnp.sum(row_grad.reshape(-1, row_count).astype(jnp.float32), axis=1)
        sum_mix = sum_mix.at[slot_flat].add(slot_grad)
        grad_hidden = (weight_col * slopes).astype(jnp.bfloat16)
        grad_down = jnp.dot(x_rows.T, grad_hidden, preferred_element_type=jnp.float32).astype(jnp.bfloat16)
        weighted = (weight_col * hidden).astype(jnp.bfloat16)
        grad_upq = jnp.dot(weighted[:, :rank_width].T, query_rows, preferred_element_type=jnp.float32).astype(jnp.bfloat16)
        grad_upv = jnp.dot(weighted[:, rank_width:].T, value_rows, preferred_element_type=jnp.float32).astype(jnp.bfloat16)
        return (sum_query, sum_value, sum_mix), (grad_down, grad_upq, grad_upv)

    start_query = jnp.zeros(grad_query.shape, jnp.float32)
    start_value = jnp.zeros(grad_value.shape, jnp.float32)
    start_mix = jnp.zeros((block_count * slot_count,), jnp.float32)
    finals, stacked = lax.scan(adapter_step, (start_query, start_value, start_mix), (token_idx, live_rows, mixing, a_proj, b_query, b_value, slot_order))
    sum_query, sum_value, sum_mix = finals
    grad_a, grad_bq, grad_bv = stacked
    return (sum_query.astype(jnp.bfloat16), sum_value.astype(jnp.bfloat16), grad_a, grad_bq, grad_bv, sum_mix.reshape(block_count, requests, 4))
```

```python
import jax
import jax.numpy as jnp
from jax import lax
from jax.sharding import PartitionSpec as P

REQ_MOST = 5


def row_exchange(
    tokens,
    grad_query,
    grad_value,
    a_proj,
    b_query,
    b_value,
    token_request,
    req_adapter,
    req_count,
    req_mix,
):
    peer_count = lax.axis_size("expert")
    tok_count = tokens.shape[0]
    feat_width = tokens.shape[1]
    value_width = grad_value.shape[1]
    requests = req_count.shape[1]
    slot_count = 4 * requests
    per_peer = slot_count // peer_count
    row_count = REQ_MOST
    rank_width = a_proj.shape[2] // 2
    nothing = jnp.zeros((), jnp.bfloat16)
    request_of = token_request[0]
    member = (request_of[:, None] == jnp.arange(requests, dtype=jnp.int32)[None, :]).astype(
        jnp.int32
    )
    lengths = jnp.sum(member, axis=0)
    starts = jnp.cumsum(lengths) - lengths
    owners = req_adapter[0].reshape(slot_count)
    slot_ids = jnp.arange(slot_count, dtype=jnp.int32)
    earlier = (owners[:, None] == owners[None, :]) & (slot_ids[None, :] < slot_ids[:, None])
    placed = owners * per_peer + jnp.sum(earlier.astype(jnp.int32), axis=1)
    slot_order = jnp.zeros((slot_count,), jnp.int32).at[placed].set(slot_ids)
    req_index = slot_order // 4
    pick_index = slot_order % 4
    row_ids = jnp.arange(row_count, dtype=jnp.int32)
    live_rows = (row_ids[None, :] < lengths[req_index][:, None]) & (
        pick_index < req_count[0][req_index]
    )[:, None]
    token_idx = jnp.where(live_rows, starts[req_index][:, None] + row_ids[None, :], 0)
    flat_idx = token_idx.reshape(-1)
    keep_rows = live_rows.reshape(-1, 1)
    x_rows = jnp.where(keep_rows, tokens[flat_idx], nothing).reshape(
        slot_count, row_count, feat_width
    )
    query_rows = jnp.where(keep_rows, grad_query[flat_idx], nothing).reshape(
        slot_count, row_count, feat_width
    )
    value_rows = jnp.where(keep_rows, grad_value[flat_idx], nothing).reshape(
        slot_count, row_count, value_width
    )
    weights = jnp.where(live_rows, req_mix[0][req_index, pick_index][:, None], nothing)
    a_matrix = a_proj[0]
    bq_matrix = b_query[0]
    bv_matrix = b_value[0]
    contract_last = (((1,), (1,)), ((), ()))
    contract_first = (((0,), (0,)), ((), ()))
    x_recv, q_recv, v_recv, w_recv = (
        lax.all_to_all(x_rows, "expert", split_axis=0, concat_axis=0, tiled=True),
        lax.all_to_all(query_rows, "expert", split_axis=0, concat_axis=0, tiled=True),
        lax.all_to_all(value_rows, "expert", split_axis=0, concat_axis=0, tiled=True),
        lax.all_to_all(weights, "expert", split_axis=0, concat_axis=0, tiled=True),
    )
    x_flat = x_recv.reshape(-1, feat_width)
    hidden_part = jnp.dot(x_flat, a_matrix, preferred_element_type=jnp.float32)
    q_flat = q_recv.reshape(-1, feat_width)
    v_flat = v_recv.reshape(-1, value_width)
    hidden = lax.psum(hidden_part, "tensor")
    slope_part = jnp.concatenate(
        [
            lax.dot_general(q_flat, bq_matrix, contract_last, preferred_element_type=jnp.float32),
            lax.dot_general(v_flat, bv_matrix, contract_last, preferred_element_type=jnp.float32),
        ],
        axis=1,
    )
    slopes = lax.psum(slope_part, "tensor")
    hidden_bf = hidden.astype(jnp.bfloat16)
    up_query = jnp.dot(
        hidden_bf[:, :rank_width], bq_matrix, preferred_element_type=jnp.float32
    ).astype(jnp.bfloat16)
    up_value = jnp.dot(
        hidden_bf[:, rank_width:], bv_matrix, preferred_element_type=jnp.float32
    ).astype(jnp.bfloat16)
    row_grad = jnp.sum(slopes * hidden_bf.astype(jnp.float32), axis=1).astype(jnp.bfloat16)
    weight_col = w_recv.reshape(-1, 1).astype(jnp.float32)
    grad_hidden = (weight_col * slopes).astype(jnp.bfloat16)
    grad_down = lax.dot_general(
        x_flat, grad_hidden, contract_first, preferred_element_type=jnp.float32
    ).astype(jnp.bfloat16)
    weighted = (weight_col * hidden).astype(jnp.bfloat16)
    grad_upq = lax.dot_general(
        weighted[:, :rank_width], q_flat, contract_first, preferred_element_type=jnp.float32
    ).astype(jnp.bfloat16)
    grad_upv = lax.dot_general(
        weighted[:, rank_width:], v_flat, contract_first, preferred_element_type=jnp.float32
    ).astype(jnp.bfloat16)
    back_query, back_value, back_grad = (
        lax.all_to_all(
            up_query.reshape(slot_count, row_count, feat_width),
            "expert",
            split_axis=0,
            concat_axis=0,
            tiled=True,
        ),
        lax.all_to_all(
            up_value.reshape(slot_count, row_count, value_width),
            "expert",
            split_axis=0,
            concat_axis=0,
            tiled=True,
        ),
        lax.all_to_all(
            row_grad.reshape(slot_count, row_count),
            "expert",
            split_axis=0,
            concat_axis=0,
            tiled=True,
        ),
    )
    scale_col = weights.reshape(-1, 1).astype(jnp.float32)
    out_query = (
        jnp.zeros((tok_count, feat_width), jnp.float32)
        .at[flat_idx]
        .add(scale_col * back_query.reshape(-1, feat_width).astype(jnp.float32))
    )
    out_value = (
        jnp.zeros((tok_count, value_width), jnp.float32)
        .at[flat_idx]
        .add(scale_col * back_value.reshape(-1, value_width).astype(jnp.float32))
    )
    slot_grad = jnp.sum(back_grad.astype(jnp.float32), axis=1)
    grad_mix = (
        jnp.zeros((slot_count,), jnp.float32).at[slot_order].set(slot_grad).reshape(1, requests, 4)
    )
    return (
        out_query.astype(jnp.bfloat16),
        out_value.astype(jnp.bfloat16),
        grad_down[None],
        grad_upq[None],
        grad_upv[None],
        grad_mix,
    )


LINE, PAIR = 4, 2
F32, BF16 = jnp.float32, jnp.bfloat16
MID = [(2, 4), (3, 5), (4, 2), (5, 3)]
OUT = [(2, 0), (3, 1), (4, 6), (5, 7)]


def to_place(array, place):
    return lax.ppermute(array, "expert", [(i, i ^ place) for i in range(LINE * PAIR)])


def sum_cores(part):
    return part + lax.ppermute(part, "tensor", [(0, 1), (1, 0)])


def line_gather(own):
    near = to_place(own, 2)
    inner = lax.ppermute(own, "expert", MID)
    second_out = lax.ppermute(inner, "expert", OUT)
    second_mid = lax.ppermute(near, "expert", MID)
    third_out = lax.ppermute(second_mid, "expert", OUT)
    return [own, near, second_out + second_mid, third_out + inner]


def dot(a, b, over):
    return lax.dot_general(a, b, (over, ((), ())), preferred_element_type=F32)


def pair_plan(
    tokens,
    grad_query,
    grad_value,
    a_proj,
    b_query,
    b_value,
    token_request,
    req_adapter,
    req_count,
    req_mix,
):
    me = lax.axis_index("expert")
    requests = req_count.shape[1]
    rank = b_query.shape[1]
    wide = grad_query.shape[1]
    places = jnp.arange(LINE * PAIR, dtype=jnp.int32)

    member = (token_request[0][:, None] == jnp.arange(requests, dtype=jnp.int32)).astype(F32)
    used = jnp.arange(4, dtype=jnp.int32)[None, :] < req_count[0][:, None]
    picks = ((req_adapter[0] ^ me)[:, :, None] == places) & used[:, :, None]
    req_weight = jnp.sum(jnp.where(picks, req_mix[0].astype(F32)[:, :, None], 0.0), axis=1)
    weight = jnp.sum(member[:, :, None] * req_weight[None], axis=1)

    x = line_gather(tokens)
    a_other = to_place(a_proj[0], 1)
    b = line_gather(jnp.concatenate([b_query[0], b_value[0]], axis=1))
    g_own = jnp.concatenate([grad_query, grad_value], axis=1)
    g_other = to_place(g_own, 1)
    weight_other = to_place(weight[:, 1::2], 1)

    a_both = jnp.concatenate([a_proj[0], a_other], axis=1)
    x_all = jnp.concatenate(x, axis=0)
    hidden = sum_cores(dot(x_all, a_both, ((1,), (0,)))).astype(BF16)
    count = tokens.shape[0]
    rank2 = 2 * rank
    hidden_own, hidden_other = [], []
    for j in range(LINE):
        block = hidden[j * count : (j + 1) * count]
        mine = block[:, :rank2]
        hidden_own.append(to_place(mine, 2 * j) if j else mine)
        hidden_other.append(to_place(block[:, rank2:], 2 * j + 1))

    b_all = jnp.concatenate(b, axis=0)
    g_all = jnp.concatenate([g_own, g_other], axis=0)
    slope_q = dot(g_all[:, :wide], b_all[:, :wide], ((1,), (1,)))
    slope_v = dot(g_all[:, wide:], b_all[:, wide:], ((1,), (1,)))
    slopes = sum_cores(jnp.stack([slope_q.reshape(-1, LINE, rank), slope_v.reshape(-1, LINE, rank)], axis=2))
    slopes = slopes.reshape(-1, LINE, rank2)
    weights = jnp.concatenate([weight[:, 0::2], weight_other], axis=0)
    grad_hidden = (weights[:, :, None] * slopes).astype(BF16)
    from_own, from_other = [], []
    for j in range(LINE):
        mine = grad_hidden[:count, j]
        from_own.append(to_place(mine, 2 * j) if j else mine)
        from_other.append(to_place(grad_hidden[count:, j], 2 * j + 1))
    grad_cols = jnp.concatenate([jnp.concatenate(from_own, 0), jnp.concatenate(from_other, 0)], axis=1)
    grad_a_both = dot(x_all, grad_cols, ((0,), (0,)))
    grad_a = grad_a_both[:, :rank2] + to_place(grad_a_both[:, rank2:].astype(BF16), 1).astype(F32)

    hid = jnp.concatenate([jnp.stack(hidden_own, 1), jnp.stack(hidden_other, 1)], axis=0).astype(F32)
    weighted = (weights[:, :, None] * hid).astype(BF16)
    weighted_q = weighted[:, :, :rank].reshape(-1, LINE * rank)
    weighted_v = weighted[:, :, rank:].reshape(-1, LINE * rank)
    grad_bq = dot(weighted_q, g_all[:, :wide], ((0,), (0,)))
    grad_bv = dot(weighted_v, g_all[:, wide:], ((0,), (0,)))
    grad_b = jnp.concatenate([grad_bq, grad_bv], axis=1)
    grad_b_sum = grad_b[:rank]
    for j in range(1, LINE):
        grad_b_sum = grad_b_sum + to_place(grad_b[j * rank : (j + 1) * rank].astype(BF16), 2 * j).astype(F32)

    out = jnp.concatenate(
        [
            dot(weighted_q, b_all[:, :wide], ((1,), (0,))),
            dot(weighted_v, b_all[:, wide:], ((1,), (0,))),
        ],
        axis=1,
    )
    out = out[:count] + to_place(out[count:].astype(BF16), 1).astype(F32)

    row_grad = jnp.sum(slopes * hid, axis=2)
    row_grad = jnp.stack([row_grad[:count], to_place(row_grad[count:], 1)], axis=2).reshape(count, -1)
    req_grad = jnp.sum(member[:, :, None] * row_grad[:, None, :], axis=0)
    grad_mix = jnp.sum(jnp.where(picks, req_grad[:, None, :], 0.0), axis=2)
    return (
        out[:, :wide].astype(BF16),
        out[:, wide:].astype(BF16),
        grad_a.astype(BF16)[None],
        grad_b_sum[:, :wide].astype(BF16)[None],
        grad_b_sum[:, wide:].astype(BF16)[None],
        grad_mix[None],
    )


def solution(mesh):
    in_specs = (
        P(("groups", "expert"), "tensor"),
        P(("groups", "expert"), "tensor"),
        P(("groups", "expert"), "tensor"),
        P(("groups", "expert"), "tensor", None),
        P(("groups", "expert"), None, "tensor"),
        P(("groups", "expert"), None, "tensor"),
        P(("groups", "expert"), None),
        P(("groups", "expert"), None, None),
        P(("groups", "expert"), None),
        P(("groups", "expert"), None, None),
    )
    out_specs = (
        P(("groups", "expert"), "tensor"),
        P(("groups", "expert"), "tensor"),
        P(("groups", "expert"), "tensor", None),
        P(("groups", "expert"), None, "tensor"),
        P(("groups", "expert"), None, "tensor"),
        P(("groups", "expert"), None, None),
    )
    shards = pair_plan if mesh.shape["expert"] == LINE * PAIR else row_exchange
    return jax.shard_map(shards, mesh=mesh, in_specs=in_specs, out_specs=out_specs, check_vma=False)
```

```python
import jax
import jax.numpy as jnp
from jax import lax
from jax.experimental import pallas as pl
from jax.experimental.pallas import tpu as pltpu
from jax.sharding import PartitionSpec as P

REQ_MOST = 5


def row_exchange(
    tokens,
    grad_query,
    grad_value,
    a_proj,
    b_query,
    b_value,
    token_request,
    req_adapter,
    req_count,
    req_mix,
):
    peer_count = lax.axis_size("expert")
    tok_count = tokens.shape[0]
    feat_width = tokens.shape[1]
    value_width = grad_value.shape[1]
    requests = req_count.shape[1]
    slot_count = 4 * requests
    per_peer = slot_count // peer_count
    row_count = REQ_MOST
    rank_width = a_proj.shape[2] // 2
    nothing = jnp.zeros((), jnp.bfloat16)
    request_of = token_request[0]
    member = (request_of[:, None] == jnp.arange(requests, dtype=jnp.int32)[None, :]).astype(
        jnp.int32
    )
    lengths = jnp.sum(member, axis=0)
    starts = jnp.cumsum(lengths) - lengths
    owners = req_adapter[0].reshape(slot_count)
    slot_ids = jnp.arange(slot_count, dtype=jnp.int32)
    earlier = (owners[:, None] == owners[None, :]) & (slot_ids[None, :] < slot_ids[:, None])
    placed = owners * per_peer + jnp.sum(earlier.astype(jnp.int32), axis=1)
    slot_order = jnp.zeros((slot_count,), jnp.int32).at[placed].set(slot_ids)
    req_index = slot_order // 4
    pick_index = slot_order % 4
    row_ids = jnp.arange(row_count, dtype=jnp.int32)
    live_rows = (row_ids[None, :] < lengths[req_index][:, None]) & (
        pick_index < req_count[0][req_index]
    )[:, None]
    token_idx = jnp.where(live_rows, starts[req_index][:, None] + row_ids[None, :], 0)
    flat_idx = token_idx.reshape(-1)
    keep_rows = live_rows.reshape(-1, 1)
    x_rows = jnp.where(keep_rows, tokens[flat_idx], nothing).reshape(
        slot_count, row_count, feat_width
    )
    query_rows = jnp.where(keep_rows, grad_query[flat_idx], nothing).reshape(
        slot_count, row_count, feat_width
    )
    value_rows = jnp.where(keep_rows, grad_value[flat_idx], nothing).reshape(
        slot_count, row_count, value_width
    )
    weights = jnp.where(live_rows, req_mix[0][req_index, pick_index][:, None], nothing)
    a_matrix = a_proj[0]
    bq_matrix = b_query[0]
    bv_matrix = b_value[0]
    contract_last = (((1,), (1,)), ((), ()))
    contract_first = (((0,), (0,)), ((), ()))
    x_recv, q_recv, v_recv, w_recv = (
        lax.all_to_all(x_rows, "expert", split_axis=0, concat_axis=0, tiled=True),
        lax.all_to_all(query_rows, "expert", split_axis=0, concat_axis=0, tiled=True),
        lax.all_to_all(value_rows, "expert", split_axis=0, concat_axis=0, tiled=True),
        lax.all_to_all(weights, "expert", split_axis=0, concat_axis=0, tiled=True),
    )
    x_flat = x_recv.reshape(-1, feat_width)
    hidden_part = jnp.dot(x_flat, a_matrix, preferred_element_type=jnp.float32)
    q_flat = q_recv.reshape(-1, feat_width)
    v_flat = v_recv.reshape(-1, value_width)
    hidden = lax.psum(hidden_part, "tensor")
    slope_part = jnp.concatenate(
        [
            lax.dot_general(q_flat, bq_matrix, contract_last, preferred_element_type=jnp.float32),
            lax.dot_general(v_flat, bv_matrix, contract_last, preferred_element_type=jnp.float32),
        ],
        axis=1,
    )
    slopes = lax.psum(slope_part, "tensor")
    hidden_bf = hidden.astype(jnp.bfloat16)
    up_query = jnp.dot(
        hidden_bf[:, :rank_width], bq_matrix, preferred_element_type=jnp.float32
    ).astype(jnp.bfloat16)
    up_value = jnp.dot(
        hidden_bf[:, rank_width:], bv_matrix, preferred_element_type=jnp.float32
    ).astype(jnp.bfloat16)
    row_grad = jnp.sum(slopes * hidden_bf.astype(jnp.float32), axis=1).astype(jnp.bfloat16)
    weight_col = w_recv.reshape(-1, 1).astype(jnp.float32)
    grad_hidden = (weight_col * slopes).astype(jnp.bfloat16)
    grad_down = lax.dot_general(
        x_flat, grad_hidden, contract_first, preferred_element_type=jnp.float32
    ).astype(jnp.bfloat16)
    weighted = (weight_col * hidden).astype(jnp.bfloat16)
    grad_upq = lax.dot_general(
        weighted[:, :rank_width], q_flat, contract_first, preferred_element_type=jnp.float32
    ).astype(jnp.bfloat16)
    grad_upv = lax.dot_general(
        weighted[:, rank_width:], v_flat, contract_first, preferred_element_type=jnp.float32
    ).astype(jnp.bfloat16)
    back_query, back_value, back_grad = (
        lax.all_to_all(
            up_query.reshape(slot_count, row_count, feat_width),
            "expert",
            split_axis=0,
            concat_axis=0,
            tiled=True,
        ),
        lax.all_to_all(
            up_value.reshape(slot_count, row_count, value_width),
            "expert",
            split_axis=0,
            concat_axis=0,
            tiled=True,
        ),
        lax.all_to_all(
            row_grad.reshape(slot_count, row_count),
            "expert",
            split_axis=0,
            concat_axis=0,
            tiled=True,
        ),
    )
    scale_col = weights.reshape(-1, 1).astype(jnp.float32)
    out_query = (
        jnp.zeros((tok_count, feat_width), jnp.float32)
        .at[flat_idx]
        .add(scale_col * back_query.reshape(-1, feat_width).astype(jnp.float32))
    )
    out_value = (
        jnp.zeros((tok_count, value_width), jnp.float32)
        .at[flat_idx]
        .add(scale_col * back_value.reshape(-1, value_width).astype(jnp.float32))
    )
    slot_grad = jnp.sum(back_grad.astype(jnp.float32), axis=1)
    grad_mix = (
        jnp.zeros((slot_count,), jnp.float32).at[slot_order].set(slot_grad).reshape(1, requests, 4)
    )
    return (
        out_query.astype(jnp.bfloat16),
        out_value.astype(jnp.bfloat16),
        grad_down[None],
        grad_upq[None],
        grad_upv[None],
        grad_mix,
    )


LINE, PAIR = 4, 2
F32, BF16 = jnp.float32, jnp.bfloat16
MID = [(2, 4), (3, 5), (4, 2), (5, 3)]
OUT = [(2, 0), (3, 1), (4, 6), (5, 7)]
ROWS, COLS, SAME = ((0,), (0,)), ((1,), (1,)), ((1,), (0,))
LANES = 128
PREP_VMEM = 60
COST = pl.CostEstimate(flops=0, bytes_accessed=0, transcendentals=0)


def to_place(array, place):
    return lax.ppermute(array, "expert", [(i, i ^ place) for i in range(LINE * PAIR)])


def other_core(part):
    return lax.ppermute(part, "tensor", [(0, 1), (1, 0)])


def line_gather(own):
    near = to_place(own, 2)
    inner = lax.ppermute(own, "expert", MID)
    second_out = lax.ppermute(inner, "expert", OUT)
    second_mid = lax.ppermute(near, "expert", MID)
    third_out = lax.ppermute(second_mid, "expert", OUT)
    return near, second_out, second_mid, inner, third_out


def dot(a, b, over):
    return lax.dot_general(a, b, (over, ((), ())), preferred_element_type=F32)


def call(kernel, outs, *ins, vmem=24):
    shapes = [jax.ShapeDtypeStruct(shape, dtype) for shape, dtype in outs]
    return pl.pallas_call(
        kernel,
        out_shape=shapes,
        in_specs=[pl.BlockSpec(memory_space=pltpu.VMEM)] * len(ins),
        out_specs=[pl.BlockSpec(memory_space=pltpu.VMEM)] * len(outs),
        compiler_params=pltpu.CompilerParams(vmem_limit_bytes=vmem * 1024 * 1024),
        cost_estimate=COST,
    )(*ins)


def members(request_row, requests):
    tok = request_row.shape[1]
    ids = lax.broadcasted_iota(jnp.int32, (requests, tok), 0)
    return ids == jnp.broadcast_to(request_row, (requests, tok))


def picked(me_ref, ra_ref, rc_ref, k, place):
    found = (jnp.broadcast_to(ra_ref[0, k : k + 1, :], place.shape) ^ me_ref[0]) == place
    return found & jnp.broadcast_to(rc_ref[...] > k, place.shape)


def prepare(me_ref, tr, ra, rc, rm, bq, bv, gq, gv, x, a, pay_ref, gw_ref, a_ref, tr_ref, ra_ref, rc_ref, rm_ref, sems):
    count, wide = x.shape
    rank, narrow = bv.shape[1:]
    full = wide + narrow
    step = rank * narrow // wide
    pairs = [
        (tr, tr_ref),
        (ra, ra_ref),
        (rc, rc_ref),
        (rm, rm_ref),
        (x, pay_ref.at[pl.ds(0, count)]),
        (bq.at[0], pay_ref.at[pl.ds(count, rank)]),
        (gq, gw_ref.at[:, pl.ds(0, wide)]),
        (gv, gw_ref.at[:, pl.ds(wide, narrow)]),
        (a, a_ref),
    ]
    for i in range(rank // step):
        dst = pay_ref.at[pl.ds(count + rank, step), pl.ds(i * narrow, narrow)]
        pairs.append((bv.at[0, pl.ds(i * step, step)], dst))
    copies = [pltpu.make_async_copy(src, dst, sems.at[i]) for i, (src, dst) in enumerate(pairs)]
    for copy in copies:
        copy.start()
    for copy in copies[:4]:
        copy.wait()
    requests = ra_ref.shape[2]
    place = lax.broadcasted_iota(jnp.int32, (LANES, requests), 0)
    total = jnp.zeros((LANES, requests), F32)
    for k in range(4):
        mix = jnp.broadcast_to(rm_ref[0, k : k + 1, :].astype(F32), place.shape)
        total = total + jnp.where(picked(me_ref, ra_ref, rc_ref, k, place), mix, 0.0)
    high = total.astype(BF16)
    low = (total - high.astype(F32)).astype(BF16)
    member = jnp.where(members(tr_ref[...], requests), 1.0, 0.0).astype(BF16)
    gw_ref[:, full : full + LANES] = dot(member, high, ((0,), (1,))).astype(BF16)
    gw_ref[:, full + LANES :] = dot(member, low, ((0,), (1,))).astype(BF16)
    for copy in copies[4:]:
        copy.wait()


def weight_of(gw_ref, place):
    full = gw_ref.shape[1] - 2 * LANES
    high = gw_ref[:, full : full + LANES][:, place : place + 1].astype(F32)
    low = gw_ref[:, full + LANES :][:, place : place + 1].astype(F32)
    return high + low


def parts_of(pay_ref, narrow):
    rows, wide = pay_ref.shape
    blocks = wide // narrow
    step = (rows - LANES) // (blocks + 1)
    rank = blocks * step
    count = rows - rank - step
    last = pay_ref[count + rank :, :]
    value = jnp.concatenate([last[:, i * narrow : (i + 1) * narrow] for i in range(blocks)], axis=0)
    return pay_ref[:count, :], pay_ref[count : count + rank, :], value


def products(pay_refs, a_ref, ax_ref, gw_ref, gx_ref, out_ref):
    rank2 = a_ref.shape[1]
    full = gw_ref.shape[1] - 2 * LANES
    wide = pay_refs[0].shape[1]
    for j, pay_ref in enumerate(pay_refs):
        x, bq, bv = parts_of(pay_ref, full - wide)
        rows = slice(j * x.shape[0], (j + 1) * x.shape[0])
        out_ref[rows, :rank2] = dot(x, a_ref[...], SAME)
        out_ref[rows, rank2 : 2 * rank2] = dot(x, ax_ref[...], SAME)
        for i, g_ref in enumerate((gw_ref, gx_ref)):
            part_q = dot(g_ref[:, :wide], bq, COLS)
            part_v = dot(g_ref[:, wide:full], bv, COLS)
            cols = slice((2 + i) * rank2, (3 + i) * rank2)
            out_ref[rows, cols] = jnp.concatenate([part_q, part_v], axis=1)


def products_early(own, near, out2, mid2, a_ref, ax_ref, gw_ref, gx_ref, out_ref, second_ref):
    second_ref[...] = out2[...] + mid2[...]
    products((own, near, second_ref), a_ref, ax_ref, gw_ref, gx_ref, out_ref)


def products_late(inner, out3, a_ref, ax_ref, gw_ref, gx_ref, out_ref, third_ref):
    third_ref[...] = inner[...] + out3[...]
    products((third_ref,), a_ref, ax_ref, gw_ref, gx_ref, out_ref)


def split_early(m_ref, r_ref, gw_ref, gx_ref, e0, e1, e2, sl_ref, c_ref, d_ref):
    count = e0.shape[0]
    rank2 = e0.shape[1] // 2
    for j, e in enumerate((e0, e1, e2)):
        rows = slice(j * count, (j + 1) * count)
        cols = slice(j * rank2, (j + 1) * rank2)
        total = m_ref[rows, :] + r_ref[rows, :]
        e[...] = total[:, : 2 * rank2].astype(BF16)
        sl_ref[rows, :] = total[:, 2 * rank2 :]
        c_ref[:, cols] = (weight_of(gw_ref, 2 * j) * total[:, 2 * rank2 : 3 * rank2]).astype(BF16)
        d_ref[:, cols] = (weight_of(gx_ref, 2 * j + 1) * total[:, 3 * rank2 :]).astype(BF16)


def pack_early(e0, e1, e2, c_ref, d_ref, t_ref, q0, q1, q2):
    rank2 = e0.shape[1] // 2
    for j, (e, q) in enumerate(((e0, q0), (e1, q1), (e2, q2))):
        cols = slice(j * rank2, (j + 1) * rank2)
        t_ref[:, cols] = e[:, rank2:]
        q[:, :rank2] = c_ref[:, cols]
        q[:, rank2:] = d_ref[:, cols]


def split_late(m_ref, r_ref, gw_ref, gx_ref, sl_ref, near_ref, far_ref):
    rank2 = near_ref.shape[1] // 2
    total = m_ref[...] + r_ref[...]
    sl_ref[...] = total[:, 2 * rank2 :]
    near_ref[:, :rank2] = total[:, :rank2].astype(BF16)
    far_ref[:, :rank2] = total[:, rank2 : 2 * rank2].astype(BF16)
    near_ref[:, rank2:] = (weight_of(gw_ref, 6) * total[:, 2 * rank2 : 3 * rank2]).astype(BF16)
    far_ref[:, rank2:] = (weight_of(gx_ref, 7) * total[:, 3 * rank2 :]).astype(BF16)


def grad_b_part(first, owns, others, gw_ref, gx_ref, wt_ref, p_refs):
    count = gw_ref.shape[0]
    rank2 = 2 * p_refs[0].shape[0]
    rank = rank2 // 2
    full = p_refs[0].shape[1]
    wide = full - full // 5
    for j, (own, other) in enumerate(zip(owns, others)):
        cols = slice(j * rank2, (j + 1) * rank2)
        own = weight_of(gw_ref, 2 * (first + j)) * own.astype(F32)
        other = weight_of(gx_ref, 2 * (first + j) + 1) * other.astype(F32)
        wt_ref[:count, cols] = own.astype(BF16)
        wt_ref[count:, cols] = other.astype(BF16)
    slots = len(p_refs)
    left = [j * rank2 + i * rank for i in range(2) for j in range(slots)]
    both = wt_ref[...]
    both = jnp.concatenate([both[:, c : c + rank] for c in left], axis=1)
    own, other = both[:count], both[count:]
    half = slots * rank
    part_q = dot(own[:, :half], gw_ref[:, :wide], ROWS) + dot(other[:, :half], gx_ref[:, :wide], ROWS)
    part_v = dot(own[:, half:], gw_ref[:, wide:full], ROWS) + dot(other[:, half:], gx_ref[:, wide:full], ROWS)
    for j, p_ref in enumerate(p_refs):
        p_ref[:, :wide] = part_q[j * rank : (j + 1) * rank].astype(p_ref.dtype)
        p_ref[:, wide:] = part_v[j * rank : (j + 1) * rank].astype(p_ref.dtype)


def grad_b_early(e0, e1, e2, t_ref, gw_ref, gx_ref, wt_ref, p0, p1, p2):
    rank2 = e0.shape[1] // 2
    owns = [e[:, :rank2] for e in (e0, e1, e2)]
    others = [t_ref[:, j * rank2 : (j + 1) * rank2] for j in range(3)]
    grad_b_part(0, owns, others, gw_ref, gx_ref, wt_ref, (p0, p1, p2))


def grad_b_late(near_ref, far_ref, gw_ref, gx_ref, wt_ref, p3):
    rank2 = near_ref.shape[1] // 2
    grad_b_part(3, (near_ref[:, :rank2],), (far_ref[:, :rank2],), gw_ref, gx_ref, wt_ref, (p3,))


def grad_b_near(p0, p1, p2, sum_ref):
    sum_ref[...] = p0[...] + p1[...].astype(F32) + p2[...].astype(F32)


def grad_b_sum(near_ref, p3, q_ref, v_ref):
    wide = q_ref.shape[2]
    total = near_ref[...] + p3[...].astype(F32)
    q_ref[0] = total[:, :wide].astype(BF16)
    v_ref[0] = total[:, wide:].astype(BF16)


def outputs_part(wt_ref, wt3_ref, b0, b1, b2, b3, s_ref, s3_ref, e0, e1, e2, t_ref, near, far, own_ref, sent_ref, rg_ref):
    count, full = own_ref.shape
    wide = b0.shape[1]
    parts = [parts_of(b, full - wide) for b in (b0, b1, b2, b3)]
    bq = jnp.concatenate([part[1] for part in parts], axis=0)
    bv = jnp.concatenate([part[2] for part in parts], axis=0)
    rank = bq.shape[0] // LINE
    rank2 = 2 * rank
    both = jnp.concatenate([wt_ref[...], wt3_ref[...]], axis=1)
    q = jnp.concatenate([both[:, j * rank2 : j * rank2 + rank] for j in range(LINE)], axis=1)
    v = jnp.concatenate([both[:, j * rank2 + rank : (j + 1) * rank2] for j in range(LINE)], axis=1)
    out_q = dot(q, bq, SAME)
    out_v = dot(v, bv, SAME)
    own_ref[:, :wide] = out_q[:count]
    own_ref[:, wide:] = out_v[:count]
    sent_ref[:, :wide] = out_q[count:].astype(BF16)
    sent_ref[:, wide:full] = out_v[count:].astype(BF16)
    lane = lax.broadcasted_iota(jnp.int32, (count, LANES), 1)
    owns = [e[:, :rank2] for e in (e0, e1, e2, near)]
    others = [t_ref[:, j * rank2 : (j + 1) * rank2] for j in range(3)] + [far[:, :rank2]]
    for i, hid in enumerate((owns, others)):
        cols = slice(i * rank2, (i + 1) * rank2)
        found = jnp.zeros((count, LANES), F32)
        for j in range(LINE):
            slope = s_ref[j * count : (j + 1) * count, cols] if j < 3 else s3_ref[:, cols]
            grad = jnp.sum(slope * hid[j].astype(F32), axis=1, keepdims=True)
            found = jnp.where(lane == 2 * j + i, jnp.broadcast_to(grad, found.shape), found)
        if i == 0:
            rg_ref[...] = found.astype(BF16)
        else:
            sent_ref[:, full:] = found.astype(BF16)


def outputs_sum(me_ref, own_ref, sent_ref, rg_ref, tr_ref, ra_ref, rc_ref, q_ref, v_ref, mix_ref):
    full = own_ref.shape[1]
    wide = q_ref.shape[1]
    total = own_ref[...] + sent_ref[:, :full].astype(F32)
    q_ref[...] = total[:, :wide].astype(BF16)
    v_ref[...] = total[:, wide:].astype(BF16)
    requests = ra_ref.shape[2]
    row_grad = rg_ref[...] + sent_ref[:, full:]
    member = jnp.where(members(tr_ref[...], requests), 1.0, 0.0).astype(BF16)
    req_grad = dot(row_grad, member, ((0,), (1,)))
    place = lax.broadcasted_iota(jnp.int32, (LANES, requests), 0)
    for k in range(4):
        found = jnp.where(picked(me_ref, ra_ref, rc_ref, k, place), req_grad, 0.0)
        mix_ref[0, k : k + 1, :] = jnp.sum(found, axis=0, keepdims=True)


def pair_plan(
    tokens,
    grad_query,
    grad_value,
    a_proj,
    b_query,
    b_value,
    token_request,
    req_adapter,
    req_count,
    req_mix,
):
    rank = b_query.shape[1]
    rank2 = 2 * rank
    wide = grad_query.shape[1]
    full = wide + grad_value.shape[1]
    count = tokens.shape[0]
    me = lax.axis_index("expert").astype(jnp.int32).reshape(1)
    block = ((count, rank2), BF16)
    b_block = ((rank, full), BF16)
    adapters = jnp.swapaxes(req_adapter, 1, 2)
    pair = ((count, 2 * rank2), BF16)
    early = ((count, 3 * rank2), BF16)

    own, gw, a_own = call_prepare(
        me, token_request, adapters, req_count, jnp.swapaxes(req_mix, 1, 2),
        b_query, b_value, grad_query, grad_value, tokens, a_proj[0],
    )
    payload = (own.shape, BF16)
    near, inner = to_place(own, 2), lax.ppermute(own, "expert", MID)
    a_other = to_place(a_proj[0], 1)
    near, inner, a_other, gw = lax.optimization_barrier((near, inner, a_other, gw))
    out2, mid2 = lax.ppermute(inner, "expert", OUT), lax.ppermute(near, "expert", MID)
    gx = to_place(gw, 1)
    out2, mid2, gx = lax.optimization_barrier((out2, mid2, gx))
    out3 = lax.ppermute(mid2, "expert", OUT)

    m, second = call(
        products_early, [((3 * count, 4 * rank2), F32), payload], own, near, out2, mid2, a_own, a_other, gw, gx
    )
    e0, e1, e2, sl, c, d = call(
        split_early, [pair] * 3 + [((3 * count, 2 * rank2), F32), early, early], m, other_core(m), gw, gx
    )
    e1, e2, d = to_place(e1, 2), to_place(e2, 4), to_place(d, 1)
    t, q0, q1, q2 = call(pack_early, [early] + [pair] * 3, e0, e1, e2, c, d)
    (out3,) = after(t, out3)
    t, q1, q2 = to_place(t, 1), to_place(q1, 2), to_place(q2, 4)
    m3, third = call(
        products_late, [((count, 4 * rank2), F32), payload], inner, out3, a_own, a_other, gw, gx
    )
    (t,) = after(m3, t)
    wt, p0, p1, p2 = call(
        grad_b_early,
        [((2 * count, 3 * rank2), BF16), ((rank, full), F32), b_block, b_block],
        e0, e1, e2, t, gw, gx,
    )
    (m3,) = after(wt, m3)
    p1, p2 = to_place(p1, 2), to_place(p2, 4)
    sl3, z3, z7 = call(
        split_late, [((count, 2 * rank2), F32), pair, pair], m3, other_core(m3), gw, gx
    )
    (q1,) = after(sl3, q1)
    z3, z7 = to_place(z3, 6), to_place(z7, 7)
    x1, x2, x3 = near[:count], second[:count], third[:count]
    grad_a = dot(tokens, q0, ROWS) + dot(x1, q1, ROWS) + dot(x2, q2, ROWS)
    (z3,) = after(grad_a, z3)
    wt3, p3 = call(grad_b_late, [((2 * count, rank2), BF16), b_block], z3, z7, gw, gx)
    p3 = to_place(p3, 6)
    (wt,) = after(wt3, wt)
    out_own, sent, rg = call(
        outputs_part,
        [((count, full), F32), ((count, full + LANES), BF16), ((count, LANES), BF16)],
        wt, wt3, own, near, second, third, sl, sl3, e0, e1, e2, t, z3, z7,
    )
    sent = to_place(sent, 1)
    (z7,) = after(out_own, z7)
    grad_a_other = (grad_a[:, rank2:] + dot(x3, z7[:, rank2:], ROWS)).astype(BF16)
    grad_a = grad_a[:, :rank2] + dot(x3, z3[:, rank2:], ROWS)
    (p1,) = after(grad_a, p1)
    (near_sum,) = call(grad_b_near, [((rank, full), F32)], p0, p1, p2)
    (sent,) = after(near_sum, sent)
    out_query, out_value, grad_mix = call_sum(
        me, out_own, sent, rg, token_request, adapters, req_count, grad_query, grad_value
    )
    (p3,) = after(out_query, p3)
    grad_bq, grad_bv = call(grad_b_sum, [(b_query.shape, BF16), (b_value.shape, BF16)], near_sum, p3)
    (grad_a,) = after(grad_bq, grad_a)
    grad_a = grad_a + to_place(grad_a_other, 1).astype(F32)
    return out_query, out_value, grad_a.astype(BF16)[None], grad_bq, grad_bv, jnp.swapaxes(grad_mix, 1, 2)


def after(earlier, *arrays):
    return lax.optimization_barrier((*arrays, earlier))[:-1]


def call_with_me(kernel, outs, *ins):
    shapes = [jax.ShapeDtypeStruct(shape, dtype) for shape, dtype in outs]
    return pl.pallas_call(
        kernel,
        out_shape=shapes,
        in_specs=[pl.BlockSpec(memory_space=pltpu.SMEM)] + [pl.BlockSpec(memory_space=pltpu.VMEM)] * (len(ins) - 1),
        out_specs=[pl.BlockSpec(memory_space=pltpu.VMEM)] * len(outs),
        compiler_params=pltpu.CompilerParams(vmem_limit_bytes=24 * 1024 * 1024),
        cost_estimate=COST,
    )(*ins)


def call_prepare(me, *ins):
    request, adapters, counts, mix, b_query, b_value, grad_query, grad_value, x, a = ins
    rank, wide = b_query.shape[1:]
    narrow = b_value.shape[2]
    step = rank * narrow // wide
    outs = [
        (x.shape[0] + rank + step, wide),
        (grad_query.shape[0], wide + narrow + 2 * LANES),
        a.shape,
    ]
    return pl.pallas_call(
        prepare,
        out_shape=[jax.ShapeDtypeStruct(shape, BF16) for shape in outs],
        in_specs=[pl.BlockSpec(memory_space=pltpu.SMEM)] + [pl.BlockSpec(memory_space=pltpu.HBM)] * len(ins),
        out_specs=[pl.BlockSpec(memory_space=pltpu.VMEM)] * len(outs),
        scratch_shapes=[pltpu.VMEM(i.shape, i.dtype) for i in (request, adapters, counts, mix)]
        + [pltpu.SemaphoreType.DMA((len(ins) - 1 + rank // step,))],
        compiler_params=pltpu.CompilerParams(vmem_limit_bytes=PREP_VMEM * 1024 * 1024),
        cost_estimate=COST,
    )(me, *ins)


def call_sum(me, own, sent, rg, token_request, adapters, req_count, grad_query, grad_value):
    outs = [(grad_query.shape, BF16), (grad_value.shape, BF16), (adapters.shape, F32)]
    return call_with_me(outputs_sum, outs, me, own, sent, rg, token_request, adapters, req_count)


def solution(mesh):
    in_specs = (
        P(("groups", "expert"), "tensor"),
        P(("groups", "expert"), "tensor"),
        P(("groups", "expert"), "tensor"),
        P(("groups", "expert"), "tensor", None),
        P(("groups", "expert"), None, "tensor"),
        P(("groups", "expert"), None, "tensor"),
        P(("groups", "expert"), None),
        P(("groups", "expert"), None, None),
        P(("groups", "expert"), None),
        P(("groups", "expert"), None, None),
    )
    out_specs = (
        P(("groups", "expert"), "tensor"),
        P(("groups", "expert"), "tensor"),
        P(("groups", "expert"), "tensor", None),
        P(("groups", "expert"), None, "tensor"),
        P(("groups", "expert"), None, "tensor"),
        P(("groups", "expert"), None, None),
    )
    shards = pair_plan if mesh.shape["expert"] == LINE * PAIR else row_exchange
    return jax.shard_map(shards, mesh=mesh, in_specs=in_specs, out_specs=out_specs, check_vma=False)
```

```python
import functools

import jax
import jax.numpy as jnp
from jax import lax
from jax.experimental import pallas as pl
from jax.experimental.pallas import tpu as pltpu
from jax.sharding import PartitionSpec as P

REQ_MOST = 5


def row_exchange(
    tokens,
    grad_query,
    grad_value,
    a_proj,
    b_query,
    b_value,
    token_request,
    req_adapter,
    req_count,
    req_mix,
):
    peer_count = lax.axis_size("expert")
    tok_count = tokens.shape[0]
    feat_width = tokens.shape[1]
    value_width = grad_value.shape[1]
    requests = req_count.shape[1]
    slot_count = 4 * requests
    per_peer = slot_count // peer_count
    row_count = REQ_MOST
    rank_width = a_proj.shape[2] // 2
    nothing = jnp.zeros((), jnp.bfloat16)
    request_of = token_request[0]
    member = (request_of[:, None] == jnp.arange(requests, dtype=jnp.int32)[None, :]).astype(
        jnp.int32
    )
    lengths = jnp.sum(member, axis=0)
    starts = jnp.cumsum(lengths) - lengths
    owners = req_adapter[0].reshape(slot_count)
    slot_ids = jnp.arange(slot_count, dtype=jnp.int32)
    earlier = (owners[:, None] == owners[None, :]) & (slot_ids[None, :] < slot_ids[:, None])
    placed = owners * per_peer + jnp.sum(earlier.astype(jnp.int32), axis=1)
    slot_order = jnp.zeros((slot_count,), jnp.int32).at[placed].set(slot_ids)
    req_index = slot_order // 4
    pick_index = slot_order % 4
    row_ids = jnp.arange(row_count, dtype=jnp.int32)
    live_rows = (row_ids[None, :] < lengths[req_index][:, None]) & (
        pick_index < req_count[0][req_index]
    )[:, None]
    token_idx = jnp.where(live_rows, starts[req_index][:, None] + row_ids[None, :], 0)
    flat_idx = token_idx.reshape(-1)
    keep_rows = live_rows.reshape(-1, 1)
    x_rows = jnp.where(keep_rows, tokens[flat_idx], nothing).reshape(
        slot_count, row_count, feat_width
    )
    query_rows = jnp.where(keep_rows, grad_query[flat_idx], nothing).reshape(
        slot_count, row_count, feat_width
    )
    value_rows = jnp.where(keep_rows, grad_value[flat_idx], nothing).reshape(
        slot_count, row_count, value_width
    )
    weights = jnp.where(live_rows, req_mix[0][req_index, pick_index][:, None], nothing)
    a_matrix = a_proj[0]
    bq_matrix = b_query[0]
    bv_matrix = b_value[0]
    contract_last = (((1,), (1,)), ((), ()))
    contract_first = (((0,), (0,)), ((), ()))
    x_recv, q_recv, v_recv, w_recv = (
        lax.all_to_all(x_rows, "expert", split_axis=0, concat_axis=0, tiled=True),
        lax.all_to_all(query_rows, "expert", split_axis=0, concat_axis=0, tiled=True),
        lax.all_to_all(value_rows, "expert", split_axis=0, concat_axis=0, tiled=True),
        lax.all_to_all(weights, "expert", split_axis=0, concat_axis=0, tiled=True),
    )
    x_flat = x_recv.reshape(-1, feat_width)
    hidden_part = jnp.dot(x_flat, a_matrix, preferred_element_type=jnp.float32)
    q_flat = q_recv.reshape(-1, feat_width)
    v_flat = v_recv.reshape(-1, value_width)
    hidden = lax.psum(hidden_part, "tensor")
    slope_part = jnp.concatenate(
        [
            lax.dot_general(q_flat, bq_matrix, contract_last, preferred_element_type=jnp.float32),
            lax.dot_general(v_flat, bv_matrix, contract_last, preferred_element_type=jnp.float32),
        ],
        axis=1,
    )
    slopes = lax.psum(slope_part, "tensor")
    hidden_bf = hidden.astype(jnp.bfloat16)
    up_query = jnp.dot(
        hidden_bf[:, :rank_width], bq_matrix, preferred_element_type=jnp.float32
    ).astype(jnp.bfloat16)
    up_value = jnp.dot(
        hidden_bf[:, rank_width:], bv_matrix, preferred_element_type=jnp.float32
    ).astype(jnp.bfloat16)
    row_grad = jnp.sum(slopes * hidden_bf.astype(jnp.float32), axis=1).astype(jnp.bfloat16)
    weight_col = w_recv.reshape(-1, 1).astype(jnp.float32)
    grad_hidden = (weight_col * slopes).astype(jnp.bfloat16)
    grad_down = lax.dot_general(
        x_flat, grad_hidden, contract_first, preferred_element_type=jnp.float32
    ).astype(jnp.bfloat16)
    weighted = (weight_col * hidden).astype(jnp.bfloat16)
    grad_upq = lax.dot_general(
        weighted[:, :rank_width], q_flat, contract_first, preferred_element_type=jnp.float32
    ).astype(jnp.bfloat16)
    grad_upv = lax.dot_general(
        weighted[:, rank_width:], v_flat, contract_first, preferred_element_type=jnp.float32
    ).astype(jnp.bfloat16)
    back_query, back_value, back_grad = (
        lax.all_to_all(
            up_query.reshape(slot_count, row_count, feat_width),
            "expert",
            split_axis=0,
            concat_axis=0,
            tiled=True,
        ),
        lax.all_to_all(
            up_value.reshape(slot_count, row_count, value_width),
            "expert",
            split_axis=0,
            concat_axis=0,
            tiled=True,
        ),
        lax.all_to_all(
            row_grad.reshape(slot_count, row_count),
            "expert",
            split_axis=0,
            concat_axis=0,
            tiled=True,
        ),
    )
    scale_col = weights.reshape(-1, 1).astype(jnp.float32)
    out_query = (
        jnp.zeros((tok_count, feat_width), jnp.float32)
        .at[flat_idx]
        .add(scale_col * back_query.reshape(-1, feat_width).astype(jnp.float32))
    )
    out_value = (
        jnp.zeros((tok_count, value_width), jnp.float32)
        .at[flat_idx]
        .add(scale_col * back_value.reshape(-1, value_width).astype(jnp.float32))
    )
    slot_grad = jnp.sum(back_grad.astype(jnp.float32), axis=1)
    grad_mix = (
        jnp.zeros((slot_count,), jnp.float32).at[slot_order].set(slot_grad).reshape(1, requests, 4)
    )
    return (
        out_query.astype(jnp.bfloat16),
        out_value.astype(jnp.bfloat16),
        grad_down[None],
        grad_upq[None],
        grad_upv[None],
        grad_mix,
    )


LINE, PAIR = 4, 2
F32, BF16 = jnp.float32, jnp.bfloat16
MID = [(2, 4), (3, 5), (4, 2), (5, 3)]
OUT = [(2, 0), (3, 1), (4, 6), (5, 7)]
ROWS, COLS, SAME = ((0,), (0,)), ((1,), (1,)), ((1,), (0,))
LANES = 128
PREP_VMEM = 24


def cost(us):
    return pl.CostEstimate(flops=0, bytes_accessed=int(us * 3.0e6), transcendentals=0)


def to_place(array, place):
    return lax.ppermute(array, "expert", [(i, i ^ place) for i in range(LINE * PAIR)])


def other_core(part):
    return lax.ppermute(part, "tensor", [(0, 1), (1, 0)])


def line_gather(own):
    near = to_place(own, 2)
    inner = lax.ppermute(own, "expert", MID)
    second_out = lax.ppermute(inner, "expert", OUT)
    second_mid = lax.ppermute(near, "expert", MID)
    third_out = lax.ppermute(second_mid, "expert", OUT)
    return near, second_out, second_mid, inner, third_out


def dot(a, b, over):
    return lax.dot_general(a, b, (over, ((), ())), preferred_element_type=F32)


def call(kernel, outs, *ins, vmem=24, us=0):
    shapes = [jax.ShapeDtypeStruct(shape, dtype) for shape, dtype in outs]
    return pl.pallas_call(
        kernel,
        out_shape=shapes,
        in_specs=[pl.BlockSpec(memory_space=pltpu.VMEM)] * len(ins),
        out_specs=[pl.BlockSpec(memory_space=pltpu.VMEM)] * len(outs),
        compiler_params=pltpu.CompilerParams(vmem_limit_bytes=vmem * 1024 * 1024),
        cost_estimate=cost(us),
    )(*ins)


def members(request_row, requests):
    tok = request_row.shape[1]
    ids = lax.broadcasted_iota(jnp.int32, (requests, tok), 0)
    return ids == jnp.broadcast_to(request_row, (requests, tok))


def picked(me_ref, ra_ref, rc_ref, k, place):
    found = (jnp.broadcast_to(ra_ref[0, k : k + 1, :], place.shape) ^ me_ref[0]) == place
    return found & jnp.broadcast_to(rc_ref[...] > k, place.shape)


def prepare(me_ref, tr, ra, rc, rm, bq, bv, gq, gv, x, a, b_ref, gw_ref, x_ref, a_ref, tr_ref, ra_ref, rc_ref, rm_ref, sems):
    wide = x.shape[1]
    rank, narrow = bv.shape[1:]
    full = wide + narrow
    step = rank * narrow // wide
    pairs = [
        (tr, tr_ref),
        (ra, ra_ref),
        (rc, rc_ref),
        (rm, rm_ref),
        (bq.at[0], b_ref.at[pl.ds(0, rank)]),
        (gq, gw_ref.at[:, pl.ds(0, wide)]),
        (gv, gw_ref.at[:, pl.ds(wide, narrow)]),
        (x, x_ref),
        (a, a_ref),
    ]
    for i in range(rank // step):
        dst = b_ref.at[pl.ds(rank, step), pl.ds(i * narrow, narrow)]
        pairs.append((bv.at[0, pl.ds(i * step, step)], dst))
    copies = [pltpu.make_async_copy(src, dst, sems.at[i]) for i, (src, dst) in enumerate(pairs)]
    for copy in copies:
        copy.start()
    for copy in copies[:4]:
        copy.wait()
    requests = ra_ref.shape[2]
    place = lax.broadcasted_iota(jnp.int32, (LANES, requests), 0)
    total = jnp.zeros((LANES, requests), F32)
    for k in range(4):
        mix = jnp.broadcast_to(rm_ref[0, k : k + 1, :].astype(F32), place.shape)
        total = total + jnp.where(picked(me_ref, ra_ref, rc_ref, k, place), mix, 0.0)
    high = total.astype(BF16)
    low = (total - high.astype(F32)).astype(BF16)
    member = jnp.where(members(tr_ref[...], requests), 1.0, 0.0).astype(BF16)
    gw_ref[:, full : full + LANES] = dot(member, high, ((0,), (1,))).astype(BF16)
    gw_ref[:, full + LANES :] = dot(member, low, ((0,), (1,))).astype(BF16)
    for copy in copies[4:]:
        copy.wait()


def weight_of(gw_ref, place):
    full = gw_ref.shape[1] - 2 * LANES
    high = gw_ref[:, full : full + LANES][:, place : place + 1].astype(F32)
    low = gw_ref[:, full + LANES :][:, place : place + 1].astype(F32)
    return high + low


def b_parts(b, narrow):
    rows, wide = b.shape
    blocks = wide // narrow
    step = rows // (blocks + 1)
    last = b[blocks * step :, :]
    value = jnp.concatenate([last[:, i * narrow : (i + 1) * narrow] for i in range(blocks)], axis=0)
    return b[: blocks * step, :], value


def hidden_of(x, rows, a_ref, ax_ref, out_ref):
    rank2 = a_ref.shape[1]
    out_ref[rows, :rank2] = dot(x, a_ref[...], SAME)
    out_ref[rows, rank2 : 2 * rank2] = dot(x, ax_ref[...], SAME)


def slopes_of(b, rows, first, gw_ref, gx_ref, out_ref):
    full = gw_ref.shape[1] - 2 * LANES
    wide = b.shape[1]
    bq, bv = b_parts(b, full - wide)
    rank2 = 2 * bq.shape[0]
    for i, g_ref in enumerate((gw_ref, gx_ref)):
        part_q = dot(g_ref[:, :wide], bq, COLS)
        part_v = dot(g_ref[:, wide:full], bv, COLS)
        cols = slice(first + i * rank2, first + (i + 1) * rank2)
        out_ref[rows, cols] = jnp.concatenate([part_q, part_v], axis=1)


def products_early(x0, x1, xo, xm, b0, b1, bo, bm, a_ref, ax_ref, gw_ref, gx_ref, h_ref, s_ref, x2_ref, b2_ref):
    count = x2_ref.shape[0]
    x2_ref[...] = xo[...] + xm[...]
    b2_ref[...] = bo[...] + bm[...]
    for j, (x, b) in enumerate(((x0, b0), (x1, b1), (x2_ref, b2_ref))):
        rows = slice(j * count, (j + 1) * count)
        hidden_of(x[...], rows, a_ref, ax_ref, h_ref)
        slopes_of(b[...], rows, 0, gw_ref, gx_ref, s_ref)


def products_late(xi, xo, bi, bo, a_ref, ax_ref, gw_ref, gx_ref, out_ref, x3_ref, b3_ref):
    rank2 = a_ref.shape[1]
    x3_ref[...] = xi[...] + xo[...]
    b3_ref[...] = bi[...] + bo[...]
    rows = slice(0, x3_ref.shape[0])
    hidden_of(x3_ref[...], rows, a_ref, ax_ref, out_ref)
    slopes_of(b3_ref[...], rows, 2 * rank2, gw_ref, gx_ref, out_ref)


def split_early(h_ref, hr_ref, s_ref, sr_ref, gw_ref, gx_ref, e0, e1, e2, sl_ref, c_ref, d_ref):
    count = e0.shape[0]
    rank2 = e0.shape[1] // 2
    for j, e in enumerate((e0, e1, e2)):
        rows = slice(j * count, (j + 1) * count)
        cols = slice(j * rank2, (j + 1) * rank2)
        e[...] = (h_ref[rows, :] + hr_ref[rows, :]).astype(BF16)
        total = s_ref[rows, :] + sr_ref[rows, :]
        sl_ref[rows, :] = total
        c_ref[:, cols] = (weight_of(gw_ref, 2 * j) * total[:, :rank2]).astype(BF16)
        d_ref[:, cols] = (weight_of(gx_ref, 2 * j + 1) * total[:, rank2:]).astype(BF16)


def pack_early(e0, e1, e2, c_ref, d_ref, t_ref, q0, q1, q2):
    rank2 = e0.shape[1] // 2
    for j, (e, q) in enumerate(((e0, q0), (e1, q1), (e2, q2))):
        cols = slice(j * rank2, (j + 1) * rank2)
        t_ref[:, cols] = e[:, rank2:]
        q[:, :rank2] = c_ref[:, cols]
        q[:, rank2:] = d_ref[:, cols]


def split_late(m_ref, r_ref, gw_ref, gx_ref, sl_ref, near_ref, far_ref):
    rank2 = near_ref.shape[1] // 2
    total = m_ref[...] + r_ref[...]
    sl_ref[...] = total[:, 2 * rank2 :]
    near_ref[:, :rank2] = total[:, :rank2].astype(BF16)
    far_ref[:, :rank2] = total[:, rank2 : 2 * rank2].astype(BF16)
    near_ref[:, rank2:] = (weight_of(gw_ref, 6) * total[:, 2 * rank2 : 3 * rank2]).astype(BF16)
    far_ref[:, rank2:] = (weight_of(gx_ref, 7) * total[:, 3 * rank2 :]).astype(BF16)


def grad_b_part(wide, first, owns, others, gw_ref, gx_ref, wt_ref, p_refs):
    count = gw_ref.shape[0]
    rank2 = 2 * p_refs[0].shape[0]
    rank = rank2 // 2
    full = p_refs[0].shape[1]
    for j, (own, other) in enumerate(zip(owns, others)):
        cols = slice(j * rank2, (j + 1) * rank2)
        own = weight_of(gw_ref, 2 * (first + j)) * own.astype(F32)
        other = weight_of(gx_ref, 2 * (first + j) + 1) * other.astype(F32)
        wt_ref[:count, cols] = own.astype(BF16)
        wt_ref[count:, cols] = other.astype(BF16)
    slots = len(p_refs)
    left = [j * rank2 + i * rank for i in range(2) for j in range(slots)]
    both = wt_ref[...]
    both = jnp.concatenate([both[:, c : c + rank] for c in left], axis=1)
    own, other = both[:count], both[count:]
    half = slots * rank
    part_q = dot(own[:, :half], gw_ref[:, :wide], ROWS) + dot(other[:, :half], gx_ref[:, :wide], ROWS)
    part_v = dot(own[:, half:], gw_ref[:, wide:full], ROWS) + dot(other[:, half:], gx_ref[:, wide:full], ROWS)
    for j, p_ref in enumerate(p_refs):
        p_ref[:, :wide] = part_q[j * rank : (j + 1) * rank].astype(p_ref.dtype)
        p_ref[:, wide:] = part_v[j * rank : (j + 1) * rank].astype(p_ref.dtype)


def grad_b_early(wide, e0, e1, e2, t_ref, gw_ref, gx_ref, wt_ref, p0, p1, p2):
    rank2 = e0.shape[1] // 2
    owns = [e[:, :rank2] for e in (e0, e1, e2)]
    others = [t_ref[:, j * rank2 : (j + 1) * rank2] for j in range(3)]
    grad_b_part(wide, 0, owns, others, gw_ref, gx_ref, wt_ref, (p0, p1, p2))


def grad_b_late(wide, near_ref, far_ref, gw_ref, gx_ref, wt_ref, p3):
    rank2 = near_ref.shape[1] // 2
    grad_b_part(wide, 3, (near_ref[:, :rank2],), (far_ref[:, :rank2],), gw_ref, gx_ref, wt_ref, (p3,))


def grad_b_near(p0, p1, p2, sum_ref):
    sum_ref[...] = p0[...] + p1[...].astype(F32) + p2[...].astype(F32)


def grad_b_sum(near_ref, p3, q_ref, v_ref):
    wide = q_ref.shape[2]
    total = near_ref[...] + p3[...].astype(F32)
    q_ref[0] = total[:, :wide].astype(BF16)
    v_ref[0] = total[:, wide:].astype(BF16)


def outputs_part(wt_ref, wt3_ref, b0, b1, b2, b3, s_ref, s3_ref, e0, e1, e2, t_ref, near, far, own_ref, sent_ref, rg_ref):
    count, full = own_ref.shape
    wide = b0.shape[1]
    parts = [b_parts(b[...], full - wide) for b in (b0, b1, b2, b3)]
    bq = jnp.concatenate([part[0] for part in parts], axis=0)
    bv = jnp.concatenate([part[1] for part in parts], axis=0)
    rank = bq.shape[0] // LINE
    rank2 = 2 * rank
    both = jnp.concatenate([wt_ref[...], wt3_ref[...]], axis=1)
    q = jnp.concatenate([both[:, j * rank2 : j * rank2 + rank] for j in range(LINE)], axis=1)
    v = jnp.concatenate([both[:, j * rank2 + rank : (j + 1) * rank2] for j in range(LINE)], axis=1)
    out_q = dot(q, bq, SAME)
    out_v = dot(v, bv, SAME)
    own_ref[:, :wide] = out_q[:count]
    own_ref[:, wide:] = out_v[:count]
    sent_ref[:, :wide] = out_q[count:].astype(BF16)
    sent_ref[:, wide:full] = out_v[count:].astype(BF16)
    lane = lax.broadcasted_iota(jnp.int32, (count, LANES), 1)
    owns = [e[:, :rank2] for e in (e0, e1, e2, near)]
    others = [t_ref[:, j * rank2 : (j + 1) * rank2] for j in range(3)] + [far[:, :rank2]]
    for i, hid in enumerate((owns, others)):
        cols = slice(i * rank2, (i + 1) * rank2)
        found = jnp.zeros((count, LANES), F32)
        for j in range(LINE):
            slope = s_ref[j * count : (j + 1) * count, cols] if j < 3 else s3_ref[:, cols]
            grad = jnp.sum(slope * hid[j].astype(F32), axis=1, keepdims=True)
            found = jnp.where(lane == 2 * j + i, jnp.broadcast_to(grad, found.shape), found)
        if i == 0:
            rg_ref[...] = found.astype(BF16)
        else:
            sent_ref[:, full:] = found.astype(BF16)


def outputs_sum(me_ref, own_ref, sent_ref, rg_ref, tr_ref, ra_ref, rc_ref, q_ref, v_ref, mix_ref):
    full = own_ref.shape[1]
    wide = q_ref.shape[1]
    total = own_ref[...] + sent_ref[:, :full].astype(F32)
    q_ref[...] = total[:, :wide].astype(BF16)
    v_ref[...] = total[:, wide:].astype(BF16)
    requests = ra_ref.shape[2]
    row_grad = rg_ref[...] + sent_ref[:, full:]
    member = jnp.where(members(tr_ref[...], requests), 1.0, 0.0).astype(BF16)
    req_grad = dot(row_grad, member, ((0,), (1,)))
    place = lax.broadcasted_iota(jnp.int32, (LANES, requests), 0)
    for k in range(4):
        found = jnp.where(picked(me_ref, ra_ref, rc_ref, k, place), req_grad, 0.0)
        mix_ref[0, k : k + 1, :] = jnp.sum(found, axis=0, keepdims=True)


def pair_plan(
    tokens,
    grad_query,
    grad_value,
    a_proj,
    b_query,
    b_value,
    token_request,
    req_adapter,
    req_count,
    req_mix,
):
    rank = b_query.shape[1]
    rank2 = 2 * rank
    wide = grad_query.shape[1]
    full = wide + grad_value.shape[1]
    count = tokens.shape[0]
    me = lax.axis_index("expert").astype(jnp.int32).reshape(1)
    block = ((count, rank2), BF16)
    b_block = ((rank, full), BF16)
    x_block = (tokens.shape, BF16)
    adapters = jnp.swapaxes(req_adapter, 1, 2)
    pair = ((count, 2 * rank2), BF16)
    early = ((count, 3 * rank2), BF16)

    x1, xi = to_place(tokens, 2), lax.ppermute(tokens, "expert", MID)
    a_other = to_place(a_proj[0], 1)
    b0, gw, x0, a_own = call_prepare(
        me, token_request, adapters, req_count, jnp.swapaxes(req_mix, 1, 2),
        b_query, b_value, grad_query, grad_value, tokens, a_proj[0],
    )
    b1, bi = to_place(b0, 2), lax.ppermute(b0, "expert", MID)
    x1, xi, a_other = lax.optimization_barrier((x1, xi, a_other))
    xo, xm = lax.ppermute(xi, "expert", OUT), lax.ppermute(x1, "expert", MID)
    bo, bm = lax.ppermute(bi, "expert", OUT), lax.ppermute(b1, "expert", MID)
    gx = to_place(gw, 1)
    xo3 = lax.ppermute(xm, "expert", OUT)
    bo3 = lax.ppermute(bm, "expert", OUT)

    wide_block = (b0.shape, BF16)
    m, ms, x2, b2 = call(
        products_early,
        [((3 * count, 2 * rank2), F32), ((3 * count, 2 * rank2), F32), x_block, wide_block],
        x0, x1, xo, xm, b0, b1, bo, bm, a_own, a_other, gw, gx,
    )
    e0, e1, e2, sl, c, d = call(
        split_early,
        [pair] * 3 + [((3 * count, 2 * rank2), F32), early, early],
        m, other_core(m), ms, other_core(ms), gw, gx,
    )
    e1, e2, d = to_place(e1, 2), to_place(e2, 4), to_place(d, 1)
    (xo3,) = after(e0, xo3)
    m3, x3, b3 = call(
        products_late,
        [((count, 4 * rank2), F32), x_block, wide_block],
        xi, xo3, bi, bo3, a_own, a_other, gw, gx,
    )
    (c,) = after(m3, c)
    t, q0, q1, q2 = call(pack_early, [early] + [pair] * 3, e0, e1, e2, c, d)
    t, q1, q2 = to_place(t, 1), to_place(q1, 2), to_place(q2, 4)
    m3 = after(q0, m3)[0]
    sl3, z3, z7 = call(
        split_late, [((count, 2 * rank2), F32), pair, pair], m3, other_core(m3), gw, gx
    )
    z3, z7 = to_place(z3, 6), to_place(z7, 7)
    (t,) = after(sl3, t)
    wt, p0, p1, p2 = call(
        functools.partial(grad_b_early, wide),
        [((2 * count, 3 * rank2), BF16), ((rank, full), F32), b_block, b_block],
        e0, e1, e2, t, gw, gx,
    )
    (q1,) = after(wt, q1)
    p1, p2 = to_place(p1, 2), to_place(p2, 4)
    x1s, x2s, x3s = x1, x2, x3
    grad_a = dot(x0, q0, ROWS) + dot(x1s, q1, ROWS) + dot(x2s, q2, ROWS)
    (z3,) = after(grad_a, z3)
    wt3, p3 = call(functools.partial(grad_b_late, wide), [((2 * count, rank2), BF16), b_block], z3, z7, gw, gx)
    p3 = to_place(p3, 6)
    (wt,) = after(wt3, wt)
    out_own, sent, rg = call(
        outputs_part,
        [((count, full), F32), ((count, full + LANES), BF16), ((count, LANES), BF16)],
        wt, wt3, b0, b1, b2, b3, sl, sl3, e0, e1, e2, t, z3, z7,
    )
    sent = to_place(sent, 1)
    (z7,) = after(out_own, z7)
    grad_a_other = (grad_a[:, rank2:] + dot(x3s, z7[:, rank2:], ROWS)).astype(BF16)
    grad_a = grad_a[:, :rank2] + dot(x3s, z3[:, rank2:], ROWS)
    (p1,) = after(grad_a, p1)
    (near_sum,) = call(grad_b_near, [((rank, full), F32)], p0, p1, p2)
    (sent,) = after(near_sum, sent)
    out_query, out_value, grad_mix = call_sum(
        me, out_own, sent, rg, token_request, adapters, req_count, grad_query, grad_value
    )
    (p3,) = after(out_query, p3)
    grad_bq, grad_bv = call(grad_b_sum, [(b_query.shape, BF16), (b_value.shape, BF16)], near_sum, p3)
    (grad_a,) = after(grad_bq, grad_a)
    grad_a = grad_a + to_place(grad_a_other, 1).astype(F32)
    return out_query, out_value, grad_a.astype(BF16)[None], grad_bq, grad_bv, jnp.swapaxes(grad_mix, 1, 2)


def after(earlier, *arrays):
    return lax.optimization_barrier((*arrays, earlier))[:-1]


def call_with_me(kernel, outs, *ins, us=0):
    shapes = [jax.ShapeDtypeStruct(shape, dtype) for shape, dtype in outs]
    return pl.pallas_call(
        kernel,
        out_shape=shapes,
        in_specs=[pl.BlockSpec(memory_space=pltpu.SMEM)] + [pl.BlockSpec(memory_space=pltpu.VMEM)] * (len(ins) - 1),
        out_specs=[pl.BlockSpec(memory_space=pltpu.VMEM)] * len(outs),
        compiler_params=pltpu.CompilerParams(vmem_limit_bytes=24 * 1024 * 1024),
        cost_estimate=cost(us),
    )(*ins)


def call_prepare(me, *ins):
    request, adapters, counts, mix, b_query, b_value, grad_query, grad_value, x, a = ins
    rank, wide = b_query.shape[1:]
    narrow = b_value.shape[2]
    step = rank * narrow // wide
    outs = [
        (rank + step, wide),
        (grad_query.shape[0], wide + narrow + 2 * LANES),
        x.shape,
        a.shape,
    ]
    return pl.pallas_call(
        prepare,
        out_shape=[jax.ShapeDtypeStruct(shape, BF16) for shape in outs],
        in_specs=[pl.BlockSpec(memory_space=pltpu.SMEM)] + [pl.BlockSpec(memory_space=pltpu.HBM)] * len(ins),
        out_specs=[pl.BlockSpec(memory_space=pltpu.VMEM)] * len(outs),
        scratch_shapes=[pltpu.VMEM(i.shape, i.dtype) for i in (request, adapters, counts, mix)]
        + [pltpu.SemaphoreType.DMA((len(ins) - 1 + rank // step,))],
        compiler_params=pltpu.CompilerParams(vmem_limit_bytes=PREP_VMEM * 1024 * 1024),
        cost_estimate=cost(0),
    )(me, *ins)


def call_sum(me, own, sent, rg, token_request, adapters, req_count, grad_query, grad_value):
    outs = [(grad_query.shape, BF16), (grad_value.shape, BF16), (adapters.shape, F32)]
    return call_with_me(outputs_sum, outs, me, own, sent, rg, token_request, adapters, req_count, us=0)


def solution(mesh):
    in_specs = (
        P(("groups", "expert"), "tensor"),
        P(("groups", "expert"), "tensor"),
        P(("groups", "expert"), "tensor"),
        P(("groups", "expert"), "tensor", None),
        P(("groups", "expert"), None, "tensor"),
        P(("groups", "expert"), None, "tensor"),
        P(("groups", "expert"), None),
        P(("groups", "expert"), None, None),
        P(("groups", "expert"), None),
        P(("groups", "expert"), None, None),
    )
    out_specs = (
        P(("groups", "expert"), "tensor"),
        P(("groups", "expert"), "tensor"),
        P(("groups", "expert"), "tensor", None),
        P(("groups", "expert"), None, "tensor"),
        P(("groups", "expert"), None, "tensor"),
        P(("groups", "expert"), None, None),
    )
    shards = pair_plan if mesh.shape["expert"] == LINE * PAIR else row_exchange
    return jax.shard_map(shards, mesh=mesh, in_specs=in_specs, out_specs=out_specs, check_vma=False)
```

```python
import functools

import jax
import jax.numpy as jnp
from jax import lax
from jax.experimental import pallas as pl
from jax.experimental.pallas import tpu as pltpu
from jax.sharding import PartitionSpec as P

REQ_MOST = 5


def row_exchange(
    tokens,
    grad_query,
    grad_value,
    a_proj,
    b_query,
    b_value,
    token_request,
    req_adapter,
    req_count,
    req_mix,
):
    peer_count = lax.axis_size("expert")
    tok_count = tokens.shape[0]
    feat_width = tokens.shape[1]
    value_width = grad_value.shape[1]
    requests = req_count.shape[1]
    slot_count = 4 * requests
    per_peer = slot_count // peer_count
    row_count = REQ_MOST
    rank_width = a_proj.shape[2] // 2
    nothing = jnp.zeros((), jnp.bfloat16)
    request_of = token_request[0]
    member = (request_of[:, None] == jnp.arange(requests, dtype=jnp.int32)[None, :]).astype(
        jnp.int32
    )
    lengths = jnp.sum(member, axis=0)
    starts = jnp.cumsum(lengths) - lengths
    owners = req_adapter[0].reshape(slot_count)
    slot_ids = jnp.arange(slot_count, dtype=jnp.int32)
    earlier = (owners[:, None] == owners[None, :]) & (slot_ids[None, :] < slot_ids[:, None])
    placed = owners * per_peer + jnp.sum(earlier.astype(jnp.int32), axis=1)
    slot_order = jnp.zeros((slot_count,), jnp.int32).at[placed].set(slot_ids)
    req_index = slot_order // 4
    pick_index = slot_order % 4
    row_ids = jnp.arange(row_count, dtype=jnp.int32)
    live_rows = (row_ids[None, :] < lengths[req_index][:, None]) & (
        pick_index < req_count[0][req_index]
    )[:, None]
    token_idx = jnp.where(live_rows, starts[req_index][:, None] + row_ids[None, :], 0)
    flat_idx = token_idx.reshape(-1)
    keep_rows = live_rows.reshape(-1, 1)
    x_rows = jnp.where(keep_rows, tokens[flat_idx], nothing).reshape(
        slot_count, row_count, feat_width
    )
    query_rows = jnp.where(keep_rows, grad_query[flat_idx], nothing).reshape(
        slot_count, row_count, feat_width
    )
    value_rows = jnp.where(keep_rows, grad_value[flat_idx], nothing).reshape(
        slot_count, row_count, value_width
    )
    weights = jnp.where(live_rows, req_mix[0][req_index, pick_index][:, None], nothing)
    a_matrix = a_proj[0]
    bq_matrix = b_query[0]
    bv_matrix = b_value[0]
    contract_last = (((1,), (1,)), ((), ()))
    contract_first = (((0,), (0,)), ((), ()))
    x_recv, q_recv, v_recv, w_recv = (
        lax.all_to_all(x_rows, "expert", split_axis=0, concat_axis=0, tiled=True),
        lax.all_to_all(query_rows, "expert", split_axis=0, concat_axis=0, tiled=True),
        lax.all_to_all(value_rows, "expert", split_axis=0, concat_axis=0, tiled=True),
        lax.all_to_all(weights, "expert", split_axis=0, concat_axis=0, tiled=True),
    )
    x_flat = x_recv.reshape(-1, feat_width)
    hidden_part = jnp.dot(x_flat, a_matrix, preferred_element_type=jnp.float32)
    q_flat = q_recv.reshape(-1, feat_width)
    v_flat = v_recv.reshape(-1, value_width)
    hidden = lax.psum(hidden_part, "tensor")
    slope_part = jnp.concatenate(
        [
            lax.dot_general(q_flat, bq_matrix, contract_last, preferred_element_type=jnp.float32),
            lax.dot_general(v_flat, bv_matrix, contract_last, preferred_element_type=jnp.float32),
        ],
        axis=1,
    )
    slopes = lax.psum(slope_part, "tensor")
    hidden_bf = hidden.astype(jnp.bfloat16)
    up_query = jnp.dot(
        hidden_bf[:, :rank_width], bq_matrix, preferred_element_type=jnp.float32
    ).astype(jnp.bfloat16)
    up_value = jnp.dot(
        hidden_bf[:, rank_width:], bv_matrix, preferred_element_type=jnp.float32
    ).astype(jnp.bfloat16)
    row_grad = jnp.sum(slopes * hidden_bf.astype(jnp.float32), axis=1).astype(jnp.bfloat16)
    weight_col = w_recv.reshape(-1, 1).astype(jnp.float32)
    grad_hidden = (weight_col * slopes).astype(jnp.bfloat16)
    grad_down = lax.dot_general(
        x_flat, grad_hidden, contract_first, preferred_element_type=jnp.float32
    ).astype(jnp.bfloat16)
    weighted = (weight_col * hidden).astype(jnp.bfloat16)
    grad_upq = lax.dot_general(
        weighted[:, :rank_width], q_flat, contract_first, preferred_element_type=jnp.float32
    ).astype(jnp.bfloat16)
    grad_upv = lax.dot_general(
        weighted[:, rank_width:], v_flat, contract_first, preferred_element_type=jnp.float32
    ).astype(jnp.bfloat16)
    back_query, back_value, back_grad = (
        lax.all_to_all(
            up_query.reshape(slot_count, row_count, feat_width),
            "expert",
            split_axis=0,
            concat_axis=0,
            tiled=True,
        ),
        lax.all_to_all(
            up_value.reshape(slot_count, row_count, value_width),
            "expert",
            split_axis=0,
            concat_axis=0,
            tiled=True,
        ),
        lax.all_to_all(
            row_grad.reshape(slot_count, row_count),
            "expert",
            split_axis=0,
            concat_axis=0,
            tiled=True,
        ),
    )
    scale_col = weights.reshape(-1, 1).astype(jnp.float32)
    out_query = (
        jnp.zeros((tok_count, feat_width), jnp.float32)
        .at[flat_idx]
        .add(scale_col * back_query.reshape(-1, feat_width).astype(jnp.float32))
    )
    out_value = (
        jnp.zeros((tok_count, value_width), jnp.float32)
        .at[flat_idx]
        .add(scale_col * back_value.reshape(-1, value_width).astype(jnp.float32))
    )
    slot_grad = jnp.sum(back_grad.astype(jnp.float32), axis=1)
    grad_mix = (
        jnp.zeros((slot_count,), jnp.float32).at[slot_order].set(slot_grad).reshape(1, requests, 4)
    )
    return (
        out_query.astype(jnp.bfloat16),
        out_value.astype(jnp.bfloat16),
        grad_down[None],
        grad_upq[None],
        grad_upv[None],
        grad_mix,
    )


LINE, PAIR = 4, 2
F32, BF16 = jnp.float32, jnp.bfloat16
MID = [(2, 4), (3, 5), (4, 2), (5, 3)]
OUT = [(2, 0), (3, 1), (4, 6), (5, 7)]
ROWS, COLS, SAME = ((0,), (0,)), ((1,), (1,)), ((1,), (0,))
LANES = 128
PREP_VMEM = 24


def cost(us):
    return pl.CostEstimate(flops=0, bytes_accessed=int(us * 3.0e6), transcendentals=0)


def to_place(array, place):
    return lax.ppermute(array, "expert", [(i, i ^ place) for i in range(LINE * PAIR)])


def other_core(part):
    return lax.ppermute(part, "tensor", [(0, 1), (1, 0)])


def line_gather(own):
    near = to_place(own, 2)
    inner = lax.ppermute(own, "expert", MID)
    second_out = lax.ppermute(inner, "expert", OUT)
    second_mid = lax.ppermute(near, "expert", MID)
    third_out = lax.ppermute(second_mid, "expert", OUT)
    return near, second_out, second_mid, inner, third_out


def dot(a, b, over):
    return lax.dot_general(a, b, (over, ((), ())), preferred_element_type=F32)


def call(kernel, outs, *ins, vmem=24, us=0):
    shapes = [jax.ShapeDtypeStruct(shape, dtype) for shape, dtype in outs]
    return pl.pallas_call(
        kernel,
        out_shape=shapes,
        in_specs=[pl.BlockSpec(memory_space=pltpu.VMEM)] * len(ins),
        out_specs=[pl.BlockSpec(memory_space=pltpu.VMEM)] * len(outs),
        compiler_params=pltpu.CompilerParams(vmem_limit_bytes=vmem * 1024 * 1024),
        cost_estimate=cost(us),
    )(*ins)


def members(request_row, requests):
    tok = request_row.shape[1]
    ids = lax.broadcasted_iota(jnp.int32, (requests, tok), 0)
    return ids == jnp.broadcast_to(request_row, (requests, tok))


def picked(me_ref, ra_ref, rc_ref, k, place):
    found = (jnp.broadcast_to(ra_ref[0, k : k + 1, :], place.shape) ^ me_ref[0]) == place
    return found & jnp.broadcast_to(rc_ref[...] > k, place.shape)


def prepare(me_ref, tr, ra, rc, rm, bq, bv, gq, gv, x, a, b_ref, gw_ref, x_ref, a_ref, tr_ref, ra_ref, rc_ref, rm_ref, sems):
    wide = x.shape[1]
    rank, narrow = bv.shape[1:]
    full = wide + narrow
    step = rank * narrow // wide
    pairs = [
        (tr, tr_ref),
        (ra, ra_ref),
        (rc, rc_ref),
        (rm, rm_ref),
        (bq.at[0], b_ref.at[pl.ds(0, rank)]),
        (gq, gw_ref.at[:, pl.ds(0, wide)]),
        (gv, gw_ref.at[:, pl.ds(wide, narrow)]),
        (x, x_ref),
        (a, a_ref),
    ]
    for i in range(rank // step):
        dst = b_ref.at[pl.ds(rank, step), pl.ds(i * narrow, narrow)]
        pairs.append((bv.at[0, pl.ds(i * step, step)], dst))
    copies = [pltpu.make_async_copy(src, dst, sems.at[i]) for i, (src, dst) in enumerate(pairs)]
    for copy in copies:
        copy.start()
    for copy in copies[:4]:
        copy.wait()
    requests = ra_ref.shape[2]
    place = lax.broadcasted_iota(jnp.int32, (LANES, requests), 0)
    total = jnp.zeros((LANES, requests), F32)
    for k in range(4):
        mix = jnp.broadcast_to(rm_ref[0, k : k + 1, :].astype(F32), place.shape)
        total = total + jnp.where(picked(me_ref, ra_ref, rc_ref, k, place), mix, 0.0)
    high = total.astype(BF16)
    low = (total - high.astype(F32)).astype(BF16)
    member = jnp.where(members(tr_ref[...], requests), 1.0, 0.0).astype(BF16)
    gw_ref[:, full : full + LANES] = dot(member, high, ((0,), (1,))).astype(BF16)
    gw_ref[:, full + LANES :] = dot(member, low, ((0,), (1,))).astype(BF16)
    for copy in copies[4:]:
        copy.wait()


def weight_of(gw_ref, place):
    full = gw_ref.shape[1] - 2 * LANES
    high = gw_ref[:, full : full + LANES][:, place : place + 1].astype(F32)
    low = gw_ref[:, full + LANES :][:, place : place + 1].astype(F32)
    return high + low


def b_parts(b, narrow):
    rows, wide = b.shape
    blocks = wide // narrow
    step = rows // (blocks + 1)
    last = b[blocks * step :, :]
    value = jnp.concatenate([last[:, i * narrow : (i + 1) * narrow] for i in range(blocks)], axis=0)
    return b[: blocks * step, :], value


def hidden_of(x, rows, a_ref, ax_ref, out_ref):
    rank2 = a_ref.shape[1]
    out_ref[rows, :rank2] = dot(x, a_ref[...], SAME)
    out_ref[rows, rank2 : 2 * rank2] = dot(x, ax_ref[...], SAME)


def slopes_of(b, rows, first, gw_ref, gx_ref, out_ref):
    full = gw_ref.shape[1] - 2 * LANES
    wide = b.shape[1]
    bq, bv = b_parts(b, full - wide)
    rank2 = 2 * bq.shape[0]
    for i, g_ref in enumerate((gw_ref, gx_ref)):
        part_q = dot(g_ref[:, :wide], bq, COLS)
        part_v = dot(g_ref[:, wide:full], bv, COLS)
        out_ref[rows, first + i * rank2 : first + (i + 1) * rank2] = jnp.concatenate([part_q, part_v], axis=1)


def products_early(x0, x1, xo, xm, b0, b1, bo, bm, a_ref, ax_ref, gw_ref, gx_ref, h_ref, s_ref, x2_ref, b2_ref):
    count = x2_ref.shape[0]
    x2_ref[...] = xo[...] + xm[...]
    b2_ref[...] = bo[...] + bm[...]
    for j, (x, b) in enumerate(((x0, b0), (x1, b1), (x2_ref, b2_ref))):
        rows = slice(j * count, (j + 1) * count)
        hidden_of(x[...], rows, a_ref, ax_ref, h_ref)
        slopes_of(b[...], rows, 0, gw_ref, gx_ref, s_ref)


def products_late(xi, xo, bi, bo, a_ref, ax_ref, gw_ref, gx_ref, out_ref, x3_ref, b3_ref):
    x3_ref[...] = xi[...] + xo[...]
    b3_ref[...] = bi[...] + bo[...]
    rows = slice(0, x3_ref.shape[0])
    hidden_of(x3_ref[...], rows, a_ref, ax_ref, out_ref)
    slopes_of(b3_ref[...], rows, 2 * a_ref.shape[1], gw_ref, gx_ref, out_ref)


def split_early(m_ref, mr_ref, s_ref, sr_ref, gw_ref, gx_ref, sl_ref, near_ref, far_ref):
    count = gw_ref.shape[0]
    both = m_ref.shape[1]
    for j in range(LINE - 1):
        rows = slice(j * count, (j + 1) * count)
        cols = pl.ds(j * both, both)
        slope = s_ref[rows, :] + sr_ref[rows, :]
        sl_ref[rows, :] = slope
        blocks = near_ref.at[:, cols], far_ref.at[:, cols]
        fill_blocks(j, m_ref[rows, :] + mr_ref[rows, :], slope, gw_ref, gx_ref, *blocks)


def pack_slots(near_ref, far_ref, *out_refs):
    rank2 = out_refs[0].shape[1] // 4
    for j, out_ref in enumerate(out_refs):
        for half in range(2):
            first = (2 * j + half) * rank2
            out_ref[:, 2 * half * rank2 : (2 * half + 1) * rank2] = near_ref[:, first : first + rank2]
            out_ref[:, (2 * half + 1) * rank2 : (2 * half + 2) * rank2] = far_ref[:, first : first + rank2]


def split_late(m_ref, r_ref, gw_ref, gx_ref, sl_ref, near_ref, far_ref):
    total = m_ref[...] + r_ref[...]
    half = total.shape[1] // 2
    sl_ref[...] = total[:, half:]
    fill_blocks(LINE - 1, total[:, :half], total[:, half:], gw_ref, gx_ref, near_ref, far_ref)


def fill_blocks(j, hidden, slope, gw_ref, gx_ref, near_ref, far_ref):
    rank2 = near_ref.shape[1] // 2
    hidden = hidden.astype(BF16)
    near_ref[:, :rank2] = hidden[:, :rank2]
    far_ref[:, :rank2] = hidden[:, rank2:]
    near_ref[:, rank2:] = (weight_of(gw_ref, 2 * j) * slope[:, :rank2]).astype(BF16)
    far_ref[:, rank2:] = (weight_of(gx_ref, 2 * j + 1) * slope[:, rank2:]).astype(BF16)


def grad_b_parts(wide, wt_ref, gw_ref, gx_ref, *p_refs):
    count = gw_ref.shape[0]
    rank, full = p_refs[0].shape
    slots = len(p_refs)
    left = [(2 * j + i) * rank for i in range(2) for j in range(slots)]
    both = wt_ref[...]
    both = jnp.concatenate([both[:, c : c + rank] for c in left], axis=1)
    own, other = both[:count], both[count:]
    half = slots * rank
    part_q = dot(own[:, :half], gw_ref[:, :wide], ROWS) + dot(other[:, :half], gx_ref[:, :wide], ROWS)
    part_v = dot(own[:, half:], gw_ref[:, wide:full], ROWS) + dot(other[:, half:], gx_ref[:, wide:full], ROWS)
    for j, p_ref in enumerate(p_refs):
        p_ref[:, :wide] = part_q[j * rank : (j + 1) * rank].astype(p_ref.dtype)
        p_ref[:, wide:] = part_v[j * rank : (j + 1) * rank].astype(p_ref.dtype)


def grad_b_sum(p0, p1, p2, p3, q_ref, v_ref):
    wide = q_ref.shape[2]
    total = p0[...] + p1[...].astype(F32) + p2[...].astype(F32) + p3[...].astype(F32)
    q_ref[0] = total[:, :wide].astype(BF16)
    v_ref[0] = total[:, wide:].astype(BF16)


def outputs_part(
    c0, c1, c2, n3, f3, gw_ref, gx_ref, b0, b1, b2, b3, s_ref, s3_ref, own_ref, sent_ref, rg_ref, wt_ref
):
    count, full = own_ref.shape
    wide = b0.shape[1]
    parts = [b_parts(b[...], full - wide) for b in (b0, b1, b2, b3)]
    bq = jnp.concatenate([part[0] for part in parts], axis=0)
    bv = jnp.concatenate([part[1] for part in parts], axis=0)
    rank = bq.shape[0] // LINE
    rank2 = 2 * rank
    owns = [c[:, :rank2] for c in (c0, c1, c2, n3)]
    others = [c[:, rank2 : 2 * rank2] for c in (c0, c1, c2)] + [f3[:, :rank2]]
    for j in range(LINE):
        cols = slice(j * rank2, (j + 1) * rank2)
        own = weight_of(gw_ref, 2 * j) * owns[j].astype(F32)
        other = weight_of(gx_ref, 2 * j + 1) * others[j].astype(F32)
        wt_ref[:count, cols] = own.astype(BF16)
        wt_ref[count:, cols] = other.astype(BF16)
    both = wt_ref[...]
    q = jnp.concatenate([both[:, j * rank2 : j * rank2 + rank] for j in range(LINE)], axis=1)
    v = jnp.concatenate([both[:, j * rank2 + rank : (j + 1) * rank2] for j in range(LINE)], axis=1)
    out_q = dot(q, bq, SAME)
    out_v = dot(v, bv, SAME)
    own_ref[:, :wide] = out_q[:count]
    own_ref[:, wide:] = out_v[:count]
    sent_ref[:, :wide] = out_q[count:].astype(BF16)
    sent_ref[:, wide:full] = out_v[count:].astype(BF16)
    lane = lax.broadcasted_iota(jnp.int32, (count, LANES), 1)
    for i, blocks in enumerate((owns, others)):
        cols = slice(i * rank2, (i + 1) * rank2)
        found = jnp.zeros((count, LANES), F32)
        for j, block in enumerate(blocks):
            slope = s_ref[j * count : (j + 1) * count, cols] if j < 3 else s3_ref[:, cols]
            grad = jnp.sum(slope * block.astype(F32), axis=1, keepdims=True)
            found = jnp.where(lane == 2 * j + i, jnp.broadcast_to(grad, found.shape), found)
        if i == 0:
            rg_ref[...] = found.astype(BF16)
        else:
            sent_ref[:, full:] = found.astype(BF16)


def outputs_sum(me_ref, own_ref, sent_ref, rg_ref, tr_ref, ra_ref, rc_ref, q_ref, v_ref, mix_ref):
    full = own_ref.shape[1]
    wide = q_ref.shape[1]
    total = own_ref[...] + sent_ref[:, :full].astype(F32)
    q_ref[...] = total[:, :wide].astype(BF16)
    v_ref[...] = total[:, wide:].astype(BF16)
    requests = ra_ref.shape[2]
    row_grad = rg_ref[...] + sent_ref[:, full:]
    member = jnp.where(members(tr_ref[...], requests), 1.0, 0.0).astype(BF16)
    req_grad = dot(row_grad, member, ((0,), (1,)))
    place = lax.broadcasted_iota(jnp.int32, (LANES, requests), 0)
    for k in range(4):
        found = jnp.where(picked(me_ref, ra_ref, rc_ref, k, place), req_grad, 0.0)
        mix_ref[0, k : k + 1, :] = jnp.sum(found, axis=0, keepdims=True)


def pair_plan(
    tokens,
    grad_query,
    grad_value,
    a_proj,
    b_query,
    b_value,
    token_request,
    req_adapter,
    req_count,
    req_mix,
):
    rank = b_query.shape[1]
    rank2 = 2 * rank
    wide = grad_query.shape[1]
    full = wide + grad_value.shape[1]
    count = tokens.shape[0]
    me = lax.axis_index("expert").astype(jnp.int32).reshape(1)
    block = ((count, rank2), BF16)
    b_block = ((rank, full), BF16)
    x_block = (tokens.shape, BF16)
    adapters = jnp.swapaxes(req_adapter, 1, 2)
    pair = ((count, 2 * rank2), BF16)
    early = ((count, 3 * rank2), BF16)

    x1, xi = to_place(tokens, 2), lax.ppermute(tokens, "expert", MID)
    a_other = to_place(a_proj[0], 1)
    b0, gw, x0, a_own = call_prepare(
        me, token_request, adapters, req_count, jnp.swapaxes(req_mix, 1, 2),
        b_query, b_value, grad_query, grad_value, tokens, a_proj[0],
    )
    b1, bi = to_place(b0, 2), lax.ppermute(b0, "expert", MID)
    x1, xi, a_other = lax.optimization_barrier((x1, xi, a_other))
    xo, xm = lax.ppermute(xi, "expert", OUT), lax.ppermute(x1, "expert", MID)
    bo, bm = lax.ppermute(bi, "expert", OUT), lax.ppermute(b1, "expert", MID)
    gx = to_place(gw, 1)
    xo3 = lax.ppermute(xm, "expert", OUT)
    bo3 = lax.ppermute(bm, "expert", OUT)

    wide_block = (b0.shape, BF16)
    m, ms, x2, b2 = call(
        products_early,
        [((3 * count, 2 * rank2), F32), ((3 * count, 2 * rank2), F32), x_block, wide_block],
        x0, x1, xo, xm, b0, b1, bo, bm, a_own, a_other, gw, gx,
    )
    sl, near, far = call(
        split_early,
        [((3 * count, 2 * rank2), F32), ((count, 6 * rank2), BF16), ((count, 6 * rank2), BF16)],
        m, other_core(m), ms, other_core(ms), gw, gx,
    )
    near, far, xo3 = lax.optimization_barrier((near, far, xo3))
    far = to_place(far, 1)
    (bo3,) = after(far, bo3)
    c0, c1, c2 = call(pack_slots, [((count, 4 * rank2), BF16)] * 3, near, far)
    c1, c2 = to_place(c1, 2), to_place(c2, 4)
    h3, x3, b3 = call(
        products_late,
        [((count, 4 * rank2), F32), x_block, wide_block],
        xi, xo3, bi, bo3, a_own, a_other, gw, gx,
    )
    rh = other_core(h3)
    c1, c2 = after(h3, c1, c2)
    grad_a = dot(x0, c0[:, 2 * rank2 :], ROWS) + dot(x1, c1[:, 2 * rank2 :], ROWS) + dot(x2, c2[:, 2 * rank2 :], ROWS)
    rh, grad_a = lax.optimization_barrier((rh, grad_a))
    sl3, n3, f3 = call(
        split_late,
        [((count, 2 * rank2), F32), pair, pair],
        h3, rh, gw, gx,
    )
    n3, f3 = to_place(n3, 6), to_place(f3, 7)
    out_own, sent, rg, wt = call(
        outputs_part,
        [((count, full), F32), ((count, full + LANES), BF16), ((count, LANES), BF16), ((2 * count, LINE * rank2), BF16)],
        c0, c1, c2, n3, f3, gw, gx, b0, b1, b2, b3, sl, sl3,
    )
    sent = to_place(sent, 1)
    (f3s,) = after(out_own, f3)
    grad_a_other = (grad_a[:, rank2:] + dot(x3, f3s[:, rank2:], ROWS)).astype(BF16)
    (wt,) = after(grad_a_other, wt)
    p0, p1, p2, p3 = call(
        functools.partial(grad_b_parts, wide), [((rank, full), F32)] + [b_block] * 3, wt, gw, gx
    )
    p1, p2, p3 = to_place(p1, 2), to_place(p2, 4), to_place(p3, 6)
    (n3s,) = after(p0, n3)
    grad_a = grad_a[:, :rank2] + dot(x3, n3s[:, rank2:], ROWS)
    (sent,) = after(grad_a, sent)
    out_query, out_value, grad_mix = call_sum(
        me, out_own, sent, rg, token_request, adapters, req_count, grad_query, grad_value
    )
    (grad_a,) = after(out_query, grad_a)
    grad_a = grad_a + to_place(grad_a_other, 1).astype(F32)
    (p1,) = after(grad_a, p1)
    grad_bq, grad_bv = call(grad_b_sum, [(b_query.shape, BF16), (b_value.shape, BF16)], p0, p1, p2, p3)
    return out_query, out_value, grad_a.astype(BF16)[None], grad_bq, grad_bv, jnp.swapaxes(grad_mix, 1, 2)


def after(earlier, *arrays):
    return lax.optimization_barrier((*arrays, earlier))[:-1]


def call_with_me(kernel, outs, *ins, us=0):
    shapes = [jax.ShapeDtypeStruct(shape, dtype) for shape, dtype in outs]
    return pl.pallas_call(
        kernel,
        out_shape=shapes,
        in_specs=[pl.BlockSpec(memory_space=pltpu.SMEM)] + [pl.BlockSpec(memory_space=pltpu.VMEM)] * (len(ins) - 1),
        out_specs=[pl.BlockSpec(memory_space=pltpu.VMEM)] * len(outs),
        compiler_params=pltpu.CompilerParams(vmem_limit_bytes=24 * 1024 * 1024),
        cost_estimate=cost(us),
    )(*ins)


def call_prepare(me, *ins):
    request, adapters, counts, mix, b_query, b_value, grad_query, grad_value, x, a = ins
    rank, wide = b_query.shape[1:]
    narrow = b_value.shape[2]
    step = rank * narrow // wide
    outs = [
        (rank + step, wide),
        (grad_query.shape[0], wide + narrow + 2 * LANES),
        x.shape,
        a.shape,
    ]
    return pl.pallas_call(
        prepare,
        out_shape=[jax.ShapeDtypeStruct(shape, BF16) for shape in outs],
        in_specs=[pl.BlockSpec(memory_space=pltpu.SMEM)] + [pl.BlockSpec(memory_space=pltpu.HBM)] * len(ins),
        out_specs=[pl.BlockSpec(memory_space=pltpu.VMEM)] * len(outs),
        scratch_shapes=[pltpu.VMEM(i.shape, i.dtype) for i in (request, adapters, counts, mix)]
        + [pltpu.SemaphoreType.DMA((len(ins) - 1 + rank // step,))],
        compiler_params=pltpu.CompilerParams(vmem_limit_bytes=PREP_VMEM * 1024 * 1024),
        cost_estimate=cost(0),
    )(me, *ins)


def call_sum(me, own, sent, rg, token_request, adapters, req_count, grad_query, grad_value):
    outs = [(grad_query.shape, BF16), (grad_value.shape, BF16), (adapters.shape, F32)]
    return call_with_me(outputs_sum, outs, me, own, sent, rg, token_request, adapters, req_count, us=0)


def solution(mesh):
    in_specs = (
        P(("groups", "expert"), "tensor"),
        P(("groups", "expert"), "tensor"),
        P(("groups", "expert"), "tensor"),
        P(("groups", "expert"), "tensor", None),
        P(("groups", "expert"), None, "tensor"),
        P(("groups", "expert"), None, "tensor"),
        P(("groups", "expert"), None),
        P(("groups", "expert"), None, None),
        P(("groups", "expert"), None),
        P(("groups", "expert"), None, None),
    )
    out_specs = (
        P(("groups", "expert"), "tensor"),
        P(("groups", "expert"), "tensor"),
        P(("groups", "expert"), "tensor", None),
        P(("groups", "expert"), None, "tensor"),
        P(("groups", "expert"), None, "tensor"),
        P(("groups", "expert"), None, None),
    )
    shards = pair_plan if mesh.shape["expert"] == LINE * PAIR else row_exchange
    return jax.shard_map(shards, mesh=mesh, in_specs=in_specs, out_specs=out_specs, check_vma=False)
```

```python
import functools

import jax
import jax.numpy as jnp
from jax import lax
from jax.experimental import pallas as pl
from jax.experimental.pallas import tpu as pltpu
from jax.sharding import PartitionSpec as P

REQ_MOST = 5


def row_exchange(
    tokens,
    grad_query,
    grad_value,
    a_proj,
    b_query,
    b_value,
    token_request,
    req_adapter,
    req_count,
    req_mix,
):
    peer_count = lax.axis_size("expert")
    tok_count = tokens.shape[0]
    feat_width = tokens.shape[1]
    value_width = grad_value.shape[1]
    requests = req_count.shape[1]
    slot_count = 4 * requests
    per_peer = slot_count // peer_count
    row_count = REQ_MOST
    rank_width = a_proj.shape[2] // 2
    nothing = jnp.zeros((), jnp.bfloat16)
    request_of = token_request[0]
    member = (request_of[:, None] == jnp.arange(requests, dtype=jnp.int32)[None, :]).astype(
        jnp.int32
    )
    lengths = jnp.sum(member, axis=0)
    starts = jnp.cumsum(lengths) - lengths
    owners = req_adapter[0].reshape(slot_count)
    slot_ids = jnp.arange(slot_count, dtype=jnp.int32)
    earlier = (owners[:, None] == owners[None, :]) & (slot_ids[None, :] < slot_ids[:, None])
    placed = owners * per_peer + jnp.sum(earlier.astype(jnp.int32), axis=1)
    slot_order = jnp.zeros((slot_count,), jnp.int32).at[placed].set(slot_ids)
    req_index = slot_order // 4
    pick_index = slot_order % 4
    row_ids = jnp.arange(row_count, dtype=jnp.int32)
    live_rows = (row_ids[None, :] < lengths[req_index][:, None]) & (
        pick_index < req_count[0][req_index]
    )[:, None]
    token_idx = jnp.where(live_rows, starts[req_index][:, None] + row_ids[None, :], 0)
    flat_idx = token_idx.reshape(-1)
    keep_rows = live_rows.reshape(-1, 1)
    x_rows = jnp.where(keep_rows, tokens[flat_idx], nothing).reshape(
        slot_count, row_count, feat_width
    )
    query_rows = jnp.where(keep_rows, grad_query[flat_idx], nothing).reshape(
        slot_count, row_count, feat_width
    )
    value_rows = jnp.where(keep_rows, grad_value[flat_idx], nothing).reshape(
        slot_count, row_count, value_width
    )
    weights = jnp.where(live_rows, req_mix[0][req_index, pick_index][:, None], nothing)
    a_matrix = a_proj[0]
    bq_matrix = b_query[0]
    bv_matrix = b_value[0]
    contract_last = (((1,), (1,)), ((), ()))
    contract_first = (((0,), (0,)), ((), ()))
    x_recv, q_recv, v_recv, w_recv = (
        lax.all_to_all(x_rows, "expert", split_axis=0, concat_axis=0, tiled=True),
        lax.all_to_all(query_rows, "expert", split_axis=0, concat_axis=0, tiled=True),
        lax.all_to_all(value_rows, "expert", split_axis=0, concat_axis=0, tiled=True),
        lax.all_to_all(weights, "expert", split_axis=0, concat_axis=0, tiled=True),
    )
    x_flat = x_recv.reshape(-1, feat_width)
    hidden_part = jnp.dot(x_flat, a_matrix, preferred_element_type=jnp.float32)
    q_flat = q_recv.reshape(-1, feat_width)
    v_flat = v_recv.reshape(-1, value_width)
    hidden = lax.psum(hidden_part, "tensor")
    slope_part = jnp.concatenate(
        [
            lax.dot_general(q_flat, bq_matrix, contract_last, preferred_element_type=jnp.float32),
            lax.dot_general(v_flat, bv_matrix, contract_last, preferred_element_type=jnp.float32),
        ],
        axis=1,
    )
    slopes = lax.psum(slope_part, "tensor")
    hidden_bf = hidden.astype(jnp.bfloat16)
    up_query = jnp.dot(
        hidden_bf[:, :rank_width], bq_matrix, preferred_element_type=jnp.float32
    ).astype(jnp.bfloat16)
    up_value = jnp.dot(
        hidden_bf[:, rank_width:], bv_matrix, preferred_element_type=jnp.float32
    ).astype(jnp.bfloat16)
    row_grad = jnp.sum(slopes * hidden_bf.astype(jnp.float32), axis=1).astype(jnp.bfloat16)
    weight_col = w_recv.reshape(-1, 1).astype(jnp.float32)
    grad_hidden = (weight_col * slopes).astype(jnp.bfloat16)
    grad_down = lax.dot_general(
        x_flat, grad_hidden, contract_first, preferred_element_type=jnp.float32
    ).astype(jnp.bfloat16)
    weighted = (weight_col * hidden).astype(jnp.bfloat16)
    grad_upq = lax.dot_general(
        weighted[:, :rank_width], q_flat, contract_first, preferred_element_type=jnp.float32
    ).astype(jnp.bfloat16)
    grad_upv = lax.dot_general(
        weighted[:, rank_width:], v_flat, contract_first, preferred_element_type=jnp.float32
    ).astype(jnp.bfloat16)
    back_query, back_value, back_grad = (
        lax.all_to_all(
            up_query.reshape(slot_count, row_count, feat_width),
            "expert",
            split_axis=0,
            concat_axis=0,
            tiled=True,
        ),
        lax.all_to_all(
            up_value.reshape(slot_count, row_count, value_width),
            "expert",
            split_axis=0,
            concat_axis=0,
            tiled=True,
        ),
        lax.all_to_all(
            row_grad.reshape(slot_count, row_count),
            "expert",
            split_axis=0,
            concat_axis=0,
            tiled=True,
        ),
    )
    scale_col = weights.reshape(-1, 1).astype(jnp.float32)
    out_query = (
        jnp.zeros((tok_count, feat_width), jnp.float32)
        .at[flat_idx]
        .add(scale_col * back_query.reshape(-1, feat_width).astype(jnp.float32))
    )
    out_value = (
        jnp.zeros((tok_count, value_width), jnp.float32)
        .at[flat_idx]
        .add(scale_col * back_value.reshape(-1, value_width).astype(jnp.float32))
    )
    slot_grad = jnp.sum(back_grad.astype(jnp.float32), axis=1)
    grad_mix = (
        jnp.zeros((slot_count,), jnp.float32).at[slot_order].set(slot_grad).reshape(1, requests, 4)
    )
    return (
        out_query.astype(jnp.bfloat16),
        out_value.astype(jnp.bfloat16),
        grad_down[None],
        grad_upq[None],
        grad_upv[None],
        grad_mix,
    )


LINE, PAIR = 4, 2
F32, BF16 = jnp.float32, jnp.bfloat16
MID = [(2, 4), (3, 5), (4, 2), (5, 3)]
OUT = [(2, 0), (3, 1), (4, 6), (5, 7)]
ROWS, COLS, SAME = ((0,), (0,)), ((1,), (1,)), ((1,), (0,))
LANES = 128
PREP_VMEM = 24


def cost(us):
    return pl.CostEstimate(flops=0, bytes_accessed=int(us * 3.0e6), transcendentals=0)


def to_place(array, place):
    return lax.ppermute(array, "expert", [(i, i ^ place) for i in range(LINE * PAIR)])


def other_core(part):
    return lax.ppermute(part, "tensor", [(0, 1), (1, 0)])


def line_gather(own):
    near = to_place(own, 2)
    inner = lax.ppermute(own, "expert", MID)
    second_out = lax.ppermute(inner, "expert", OUT)
    second_mid = lax.ppermute(near, "expert", MID)
    third_out = lax.ppermute(second_mid, "expert", OUT)
    return near, second_out, second_mid, inner, third_out


def dot(a, b, over):
    return lax.dot_general(a, b, (over, ((), ())), preferred_element_type=F32)


def call(kernel, outs, *ins, vmem=24, us=0):
    shapes = [jax.ShapeDtypeStruct(shape, dtype) for shape, dtype in outs]
    return pl.pallas_call(
        kernel,
        out_shape=shapes,
        in_specs=[pl.BlockSpec(memory_space=pltpu.VMEM)] * len(ins),
        out_specs=[pl.BlockSpec(memory_space=pltpu.VMEM)] * len(outs),
        compiler_params=pltpu.CompilerParams(vmem_limit_bytes=vmem * 1024 * 1024),
        cost_estimate=cost(us),
    )(*ins)


def members(request_row, requests):
    tok = request_row.shape[1]
    ids = lax.broadcasted_iota(jnp.int32, (requests, tok), 0)
    return ids == jnp.broadcast_to(request_row, (requests, tok))


def picked(me_ref, ra_ref, rc_ref, k, place):
    found = (jnp.broadcast_to(ra_ref[0, k : k + 1, :], place.shape) ^ me_ref[0]) == place
    return found & jnp.broadcast_to(rc_ref[...] > k, place.shape)


def prepare(me_ref, tr, ra, rc, rm, bq, bv, gq, gv, x, a, b_ref, gw_ref, x_ref, a_ref, tr_ref, ra_ref, rc_ref, rm_ref, sems):
    wide = x.shape[1]
    rank, narrow = bv.shape[1:]
    full = wide + narrow
    step = rank * narrow // wide
    pairs = [
        (tr, tr_ref),
        (ra, ra_ref),
        (rc, rc_ref),
        (rm, rm_ref),
        (bq.at[0], b_ref.at[pl.ds(0, rank)]),
        (gq, gw_ref.at[:, pl.ds(0, wide)]),
        (gv, gw_ref.at[:, pl.ds(wide, narrow)]),
        (x, x_ref),
        (a, a_ref),
    ]
    for i in range(rank // step):
        dst = b_ref.at[pl.ds(rank, step), pl.ds(i * narrow, narrow)]
        pairs.append((bv.at[0, pl.ds(i * step, step)], dst))
    copies = [pltpu.make_async_copy(src, dst, sems.at[i]) for i, (src, dst) in enumerate(pairs)]
    for copy in copies:
        copy.start()
    for copy in copies[:4]:
        copy.wait()
    requests = ra_ref.shape[2]
    place = lax.broadcasted_iota(jnp.int32, (LANES, requests), 0)
    total = jnp.zeros((LANES, requests), F32)
    for k in range(4):
        mix = jnp.broadcast_to(rm_ref[0, k : k + 1, :].astype(F32), place.shape)
        total = total + jnp.where(picked(me_ref, ra_ref, rc_ref, k, place), mix, 0.0)
    high = total.astype(BF16)
    low = (total - high.astype(F32)).astype(BF16)
    member = jnp.where(members(tr_ref[...], requests), 1.0, 0.0).astype(BF16)
    gw_ref[:, full : full + LANES] = dot(member, high, ((0,), (1,))).astype(BF16)
    gw_ref[:, full + LANES :] = dot(member, low, ((0,), (1,))).astype(BF16)
    for copy in copies[4:]:
        copy.wait()


def weight_of(gw_ref, place):
    full = gw_ref.shape[1] - 2 * LANES
    high = gw_ref[:, full : full + LANES][:, place : place + 1].astype(F32)
    low = gw_ref[:, full + LANES :][:, place : place + 1].astype(F32)
    return high + low


def b_parts(b, narrow):
    rows, wide = b.shape
    blocks = wide // narrow
    step = rows // (blocks + 1)
    last = b[blocks * step :, :]
    value = jnp.concatenate([last[:, i * narrow : (i + 1) * narrow] for i in range(blocks)], axis=0)
    return b[: blocks * step, :], value


def hidden_of(x, rows, a_ref, ax_ref, out_ref):
    rank2 = a_ref.shape[1]
    out_ref[rows, :rank2] = dot(x, a_ref[...], SAME).astype(out_ref.dtype)
    out_ref[rows, rank2 : 2 * rank2] = dot(x, ax_ref[...], SAME).astype(out_ref.dtype)


def slopes_of(b, rows, first, gw_ref, gx_ref, out_ref):
    full = gw_ref.shape[1] - 2 * LANES
    wide = b.shape[1]
    bq, bv = b_parts(b, full - wide)
    rank2 = 2 * bq.shape[0]
    for i, g_ref in enumerate((gw_ref, gx_ref)):
        part_q = dot(g_ref[:, :wide], bq, COLS)
        part_v = dot(g_ref[:, wide:full], bv, COLS)
        out_ref[rows, first + i * rank2 : first + (i + 1) * rank2] = jnp.concatenate([part_q, part_v], axis=1).astype(out_ref.dtype)


def products_early(x0, x1, xo, xm, b0, b1, bo, bm, a_ref, ax_ref, gw_ref, gx_ref, h_ref, s_ref, x2_ref, b2_ref):
    count = x2_ref.shape[0]
    x2_ref[...] = xo[...] + xm[...]
    b2_ref[...] = bo[...] + bm[...]
    for j, (x, b) in enumerate(((x0, b0), (x1, b1), (x2_ref, b2_ref))):
        rows = slice(j * count, (j + 1) * count)
        hidden_of(x[...], rows, a_ref, ax_ref, h_ref)
        slopes_of(b[...], rows, 0, gw_ref, gx_ref, s_ref)


def products_late(xi, xo, bi, bo, a_ref, ax_ref, gw_ref, gx_ref, out_ref, x3_ref, b3_ref):
    x3_ref[...] = xi[...] + xo[...]
    b3_ref[...] = bi[...] + bo[...]
    rows = slice(0, x3_ref.shape[0])
    hidden_of(x3_ref[...], rows, a_ref, ax_ref, out_ref)
    slopes_of(b3_ref[...], rows, 2 * a_ref.shape[1], gw_ref, gx_ref, out_ref)


def split_early(m_ref, mr_ref, s_ref, sr_ref, gw_ref, gx_ref, sl_ref, near_ref, *far_refs):
    count = gw_ref.shape[0]
    both = m_ref.shape[1]
    for j in range(LINE - 1):
        rows = slice(j * count, (j + 1) * count)
        cols = pl.ds(j * both, both)
        slope = s_ref[rows, :].astype(F32) + sr_ref[rows, :].astype(F32)
        sl_ref[rows, :] = slope
        blocks = near_ref.at[:, cols], far_refs[j]
        fill_blocks(j, m_ref[rows, :].astype(F32) + mr_ref[rows, :].astype(F32), slope, gw_ref, gx_ref, *blocks)


def pack_slots(near_ref, f0, f1, f2, *out_refs):
    rank2 = out_refs[0].shape[1] // 4
    for j, (far_ref, out_ref) in enumerate(zip((f0, f1, f2), out_refs)):
        for half in range(2):
            first = (2 * j + half) * rank2
            out_ref[:, 2 * half * rank2 : (2 * half + 1) * rank2] = near_ref[:, first : first + rank2]
            out_ref[:, (2 * half + 1) * rank2 : (2 * half + 2) * rank2] = far_ref[:, half * rank2 : (half + 1) * rank2]


def split_late(m_ref, r_ref, gw_ref, gx_ref, sl_ref, near_ref, far_ref):
    total = m_ref[...].astype(F32) + r_ref[...].astype(F32)
    half = total.shape[1] // 2
    sl_ref[...] = total[:, half:]
    fill_blocks(LINE - 1, total[:, :half], total[:, half:], gw_ref, gx_ref, near_ref, far_ref)


def fill_blocks(j, hidden, slope, gw_ref, gx_ref, near_ref, far_ref):
    rank2 = near_ref.shape[1] // 2
    hidden = hidden.astype(BF16)
    near_ref[:, :rank2] = hidden[:, :rank2]
    far_ref[:, :rank2] = hidden[:, rank2:]
    near_ref[:, rank2:] = (weight_of(gw_ref, 2 * j) * slope[:, :rank2]).astype(BF16)
    far_ref[:, rank2:] = (weight_of(gx_ref, 2 * j + 1) * slope[:, rank2:]).astype(BF16)


def grad_b_parts(wide, wt_ref, gw_ref, gx_ref, *p_refs):
    count = gw_ref.shape[0]
    rank, full = p_refs[0].shape
    slots = len(p_refs)
    left = [(2 * j + i) * rank for i in range(2) for j in range(slots)]
    both = wt_ref[...]
    both = jnp.concatenate([both[:, c : c + rank] for c in left], axis=1)
    own, other = both[:count], both[count:]
    half = slots * rank
    part_q = dot(own[:, :half], gw_ref[:, :wide], ROWS) + dot(other[:, :half], gx_ref[:, :wide], ROWS)
    part_v = dot(own[:, half:], gw_ref[:, wide:full], ROWS) + dot(other[:, half:], gx_ref[:, wide:full], ROWS)
    for j, p_ref in enumerate(p_refs):
        p_ref[:, :wide] = part_q[j * rank : (j + 1) * rank].astype(p_ref.dtype)
        p_ref[:, wide:] = part_v[j * rank : (j + 1) * rank].astype(p_ref.dtype)


def grad_b_sum(p0, p1, p2, p3, q_ref, v_ref):
    wide = q_ref.shape[2]
    total = p0[...] + p1[...].astype(F32) + p2[...].astype(F32) + p3[...].astype(F32)
    q_ref[0] = total[:, :wide].astype(BF16)
    v_ref[0] = total[:, wide:].astype(BF16)


def outputs_part(
    c0, c1, c2, n3, f3, gw_ref, gx_ref, b0, b1, b2, b3, s_ref, s3_ref, own_ref, sent_ref, rg_ref, wt_ref
):
    count, full = own_ref.shape
    wide = b0.shape[1]
    parts = [b_parts(b[...], full - wide) for b in (b0, b1, b2, b3)]
    bq = jnp.concatenate([part[0] for part in parts], axis=0)
    bv = jnp.concatenate([part[1] for part in parts], axis=0)
    rank = bq.shape[0] // LINE
    rank2 = 2 * rank
    owns = [c[:, :rank2] for c in (c0, c1, c2, n3)]
    others = [c[:, rank2 : 2 * rank2] for c in (c0, c1, c2)] + [f3[:, :rank2]]
    for j in range(LINE):
        cols = slice(j * rank2, (j + 1) * rank2)
        own = weight_of(gw_ref, 2 * j) * owns[j].astype(F32)
        other = weight_of(gx_ref, 2 * j + 1) * others[j].astype(F32)
        wt_ref[:count, cols] = own.astype(BF16)
        wt_ref[count:, cols] = other.astype(BF16)
    both = wt_ref[...]
    q = jnp.concatenate([both[:, j * rank2 : j * rank2 + rank] for j in range(LINE)], axis=1)
    v = jnp.concatenate([both[:, j * rank2 + rank : (j + 1) * rank2] for j in range(LINE)], axis=1)
    out_q = dot(q, bq, SAME)
    out_v = dot(v, bv, SAME)
    own_ref[:, :wide] = out_q[:count]
    own_ref[:, wide:] = out_v[:count]
    sent_ref[:, :wide] = out_q[count:].astype(BF16)
    sent_ref[:, wide:full] = out_v[count:].astype(BF16)
    lane = lax.broadcasted_iota(jnp.int32, (count, LANES), 1)
    for i, blocks in enumerate((owns, others)):
        cols = slice(i * rank2, (i + 1) * rank2)
        found = jnp.zeros((count, LANES), F32)
        for j, block in enumerate(blocks):
            slope = s_ref[j * count : (j + 1) * count, cols] if j < 3 else s3_ref[:, cols]
            grad = jnp.sum(slope * block.astype(F32), axis=1, keepdims=True)
            found = jnp.where(lane == 2 * j + i, jnp.broadcast_to(grad, found.shape), found)
        if i == 0:
            rg_ref[...] = found.astype(BF16)
        else:
            sent_ref[:, full:] = found.astype(BF16)


def outputs_sum(me_ref, own_ref, sent_ref, rg_ref, tr_ref, ra_ref, rc_ref, q_ref, v_ref, mix_ref):
    full = own_ref.shape[1]
    wide = q_ref.shape[1]
    total = own_ref[...] + sent_ref[:, :full].astype(F32)
    q_ref[...] = total[:, :wide].astype(BF16)
    v_ref[...] = total[:, wide:].astype(BF16)
    requests = ra_ref.shape[2]
    row_grad = rg_ref[...] + sent_ref[:, full:]
    member = jnp.where(members(tr_ref[...], requests), 1.0, 0.0).astype(BF16)
    req_grad = dot(row_grad, member, ((0,), (1,)))
    place = lax.broadcasted_iota(jnp.int32, (LANES, requests), 0)
    for k in range(4):
        found = jnp.where(picked(me_ref, ra_ref, rc_ref, k, place), req_grad, 0.0)
        mix_ref[0, k : k + 1, :] = jnp.sum(found, axis=0, keepdims=True)


def pair_plan(
    tokens,
    grad_query,
    grad_value,
    a_proj,
    b_query,
    b_value,
    token_request,
    req_adapter,
    req_count,
    req_mix,
):
    rank = b_query.shape[1]
    rank2 = 2 * rank
    wide = grad_query.shape[1]
    full = wide + grad_value.shape[1]
    count = tokens.shape[0]
    me = lax.axis_index("expert").astype(jnp.int32).reshape(1)
    block = ((count, rank2), BF16)
    b_block = ((rank, full), BF16)
    x_block = (tokens.shape, BF16)
    adapters = jnp.swapaxes(req_adapter, 1, 2)
    pair = ((count, 2 * rank2), BF16)
    early = ((count, 3 * rank2), BF16)

    x1, xi = to_place(tokens, 2), lax.ppermute(tokens, "expert", MID)
    a_other = to_place(a_proj[0], 1)
    b0, gw, x0, a_own = call_prepare(
        me, token_request, adapters, req_count, jnp.swapaxes(req_mix, 1, 2),
        b_query, b_value, grad_query, grad_value, tokens, a_proj[0],
    )
    b1, bi = to_place(b0, 2), lax.ppermute(b0, "expert", MID)
    x1, a_other = lax.optimization_barrier((x1, a_other))
    xm = lax.ppermute(x1, "expert", MID)
    xo = lax.ppermute(xi, "expert", OUT)
    bo, bm = lax.ppermute(bi, "expert", OUT), lax.ppermute(b1, "expert", MID)
    gx = to_place(gw, 1)
    xo3 = lax.ppermute(xm, "expert", OUT)
    bo3 = lax.ppermute(bm, "expert", OUT)

    wide_block = (b0.shape, BF16)
    m, ms, x2, b2 = call(
        products_early,
        [((3 * count, 2 * rank2), BF16), ((3 * count, 2 * rank2), BF16), x_block, wide_block],
        x0, x1, xo, xm, b0, b1, bo, bm, a_own, a_other, gw, gx,
    )
    sl, near, *far = call(
        split_early,
        [((3 * count, 2 * rank2), F32), ((count, 6 * rank2), BF16)] + [pair] * 3,
        m, other_core(m), ms, other_core(ms), gw, gx,
    )
    (xo3,) = after(sl, xo3)
    far = [to_place(part, 1) for part in far]
    near, bo3 = lax.optimization_barrier((near, bo3))
    c0, c1, c2 = call(pack_slots, [((count, 4 * rank2), BF16)] * 3, near, *far)
    c1, c2 = to_place(c1, 2), to_place(c2, 4)
    h3, x3, b3 = call(
        products_late,
        [((count, 4 * rank2), BF16), x_block, wide_block],
        xi, xo3, bi, bo3, a_own, a_other, gw, gx,
    )
    rh = other_core(h3)
    c1, c2 = after(h3, c1, c2)
    grad_a = dot(x0, c0[:, 2 * rank2 :], ROWS) + dot(x1, c1[:, 2 * rank2 :], ROWS)
    rh, grad_a = lax.optimization_barrier((rh, grad_a))
    sl3, n3, f3 = call(
        split_late,
        [((count, 2 * rank2), F32), pair, pair],
        h3, rh, gw, gx,
    )
    n3, f3 = to_place(n3, 6), to_place(f3, 7)
    (c2,) = after(sl3, c2)
    grad_a = grad_a + dot(x2, c2[:, 2 * rank2 :], ROWS)
    n3, f3, grad_a = lax.optimization_barrier((n3, f3, grad_a))
    out_own, sent, rg, wt = call(
        outputs_part,
        [((count, full), F32), ((count, full + LANES), BF16), ((count, LANES), BF16), ((2 * count, LINE * rank2), BF16)],
        c0, c1, c2, n3, f3, gw, gx, b0, b1, b2, b3, sl, sl3,
    )
    sent = to_place(sent, 1)
    p0, p1, p2, p3 = call(
        functools.partial(grad_b_parts, wide), [((rank, full), F32)] + [b_block] * 3, wt, gw, gx
    )
    p1, p2, p3 = to_place(p1, 2), to_place(p2, 4), to_place(p3, 6)
    (f3s,) = after(p0, f3)
    grad_a_other = (grad_a[:, rank2:] + dot(x3, f3s[:, rank2:], ROWS)).astype(BF16)
    (n3s,) = after(grad_a_other, n3)
    grad_a = grad_a[:, :rank2] + dot(x3, n3s[:, rank2:], ROWS)
    (sent,) = after(grad_a, sent)
    out_query, out_value, grad_mix = call_sum(
        me, out_own, sent, rg, token_request, adapters, req_count, grad_query, grad_value
    )
    (grad_a,) = after(out_query, grad_a)
    grad_a = grad_a + to_place(grad_a_other, 1).astype(F32)
    (p1,) = after(grad_a, p1)
    grad_bq, grad_bv = call(grad_b_sum, [(b_query.shape, BF16), (b_value.shape, BF16)], p0, p1, p2, p3)
    return out_query, out_value, grad_a.astype(BF16)[None], grad_bq, grad_bv, jnp.swapaxes(grad_mix, 1, 2)


def after(earlier, *arrays):
    return lax.optimization_barrier((*arrays, earlier))[:-1]


def call_with_me(kernel, outs, *ins, us=0):
    shapes = [jax.ShapeDtypeStruct(shape, dtype) for shape, dtype in outs]
    return pl.pallas_call(
        kernel,
        out_shape=shapes,
        in_specs=[pl.BlockSpec(memory_space=pltpu.SMEM)] + [pl.BlockSpec(memory_space=pltpu.VMEM)] * (len(ins) - 1),
        out_specs=[pl.BlockSpec(memory_space=pltpu.VMEM)] * len(outs),
        compiler_params=pltpu.CompilerParams(vmem_limit_bytes=24 * 1024 * 1024),
        cost_estimate=cost(us),
    )(*ins)


def call_prepare(me, *ins):
    request, adapters, counts, mix, b_query, b_value, grad_query, grad_value, x, a = ins
    rank, wide = b_query.shape[1:]
    narrow = b_value.shape[2]
    step = rank * narrow // wide
    outs = [
        (rank + step, wide),
        (grad_query.shape[0], wide + narrow + 2 * LANES),
        x.shape,
        a.shape,
    ]
    return pl.pallas_call(
        prepare,
        out_shape=[jax.ShapeDtypeStruct(shape, BF16) for shape in outs],
        in_specs=[pl.BlockSpec(memory_space=pltpu.SMEM)] + [pl.BlockSpec(memory_space=pltpu.HBM)] * len(ins),
        out_specs=[pl.BlockSpec(memory_space=pltpu.VMEM)] * len(outs),
        scratch_shapes=[pltpu.VMEM(i.shape, i.dtype) for i in (request, adapters, counts, mix)]
        + [pltpu.SemaphoreType.DMA((len(ins) - 1 + rank // step,))],
        compiler_params=pltpu.CompilerParams(vmem_limit_bytes=PREP_VMEM * 1024 * 1024),
        cost_estimate=cost(0),
    )(me, *ins)


def call_sum(me, own, sent, rg, token_request, adapters, req_count, grad_query, grad_value):
    outs = [(grad_query.shape, BF16), (grad_value.shape, BF16), (adapters.shape, F32)]
    return call_with_me(outputs_sum, outs, me, own, sent, rg, token_request, adapters, req_count, us=0)


def solution(mesh):
    in_specs = (
        P(("groups", "expert"), "tensor"),
        P(("groups", "expert"), "tensor"),
        P(("groups", "expert"), "tensor"),
        P(("groups", "expert"), "tensor", None),
        P(("groups", "expert"), None, "tensor"),
        P(("groups", "expert"), None, "tensor"),
        P(("groups", "expert"), None),
        P(("groups", "expert"), None, None),
        P(("groups", "expert"), None),
        P(("groups", "expert"), None, None),
    )
    out_specs = (
        P(("groups", "expert"), "tensor"),
        P(("groups", "expert"), "tensor"),
        P(("groups", "expert"), "tensor", None),
        P(("groups", "expert"), None, "tensor"),
        P(("groups", "expert"), None, "tensor"),
        P(("groups", "expert"), None, None),
    )
    shards = pair_plan if mesh.shape["expert"] == LINE * PAIR else row_exchange
    return jax.shard_map(shards, mesh=mesh, in_specs=in_specs, out_specs=out_specs, check_vma=False)
```

```python
import functools

import jax
import jax.numpy as jnp
from jax import lax
from jax.experimental import pallas as pl
from jax.experimental.pallas import tpu as pltpu
from jax.sharding import PartitionSpec as P

REQ_MOST = 5


def row_exchange(
    tokens,
    grad_query,
    grad_value,
    a_proj,
    b_query,
    b_value,
    token_request,
    req_adapter,
    req_count,
    req_mix,
):
    peer_count = lax.axis_size("expert")
    tok_count = tokens.shape[0]
    feat_width = tokens.shape[1]
    value_width = grad_value.shape[1]
    requests = req_count.shape[1]
    slot_count = 4 * requests
    per_peer = slot_count // peer_count
    row_count = REQ_MOST
    rank_width = a_proj.shape[2] // 2
    nothing = jnp.zeros((), jnp.bfloat16)
    request_of = token_request[0]
    member = (request_of[:, None] == jnp.arange(requests, dtype=jnp.int32)[None, :]).astype(
        jnp.int32
    )
    lengths = jnp.sum(member, axis=0)
    starts = jnp.cumsum(lengths) - lengths
    owners = req_adapter[0].reshape(slot_count)
    slot_ids = jnp.arange(slot_count, dtype=jnp.int32)
    earlier = (owners[:, None] == owners[None, :]) & (slot_ids[None, :] < slot_ids[:, None])
    placed = owners * per_peer + jnp.sum(earlier.astype(jnp.int32), axis=1)
    slot_order = jnp.zeros((slot_count,), jnp.int32).at[placed].set(slot_ids)
    req_index = slot_order // 4
    pick_index = slot_order % 4
    row_ids = jnp.arange(row_count, dtype=jnp.int32)
    live_rows = (row_ids[None, :] < lengths[req_index][:, None]) & (
        pick_index < req_count[0][req_index]
    )[:, None]
    token_idx = jnp.where(live_rows, starts[req_index][:, None] + row_ids[None, :], 0)
    flat_idx = token_idx.reshape(-1)
    keep_rows = live_rows.reshape(-1, 1)
    x_rows = jnp.where(keep_rows, tokens[flat_idx], nothing).reshape(
        slot_count, row_count, feat_width
    )
    query_rows = jnp.where(keep_rows, grad_query[flat_idx], nothing).reshape(
        slot_count, row_count, feat_width
    )
    value_rows = jnp.where(keep_rows, grad_value[flat_idx], nothing).reshape(
        slot_count, row_count, value_width
    )
    weights = jnp.where(live_rows, req_mix[0][req_index, pick_index][:, None], nothing)
    a_matrix = a_proj[0]
    bq_matrix = b_query[0]
    bv_matrix = b_value[0]
    contract_last = (((1,), (1,)), ((), ()))
    contract_first = (((0,), (0,)), ((), ()))
    x_recv, q_recv, v_recv, w_recv = (
        lax.all_to_all(x_rows, "expert", split_axis=0, concat_axis=0, tiled=True),
        lax.all_to_all(query_rows, "expert", split_axis=0, concat_axis=0, tiled=True),
        lax.all_to_all(value_rows, "expert", split_axis=0, concat_axis=0, tiled=True),
        lax.all_to_all(weights, "expert", split_axis=0, concat_axis=0, tiled=True),
    )
    x_flat = x_recv.reshape(-1, feat_width)
    hidden_part = jnp.dot(x_flat, a_matrix, preferred_element_type=jnp.float32)
    q_flat = q_recv.reshape(-1, feat_width)
    v_flat = v_recv.reshape(-1, value_width)
    hidden = lax.psum(hidden_part, "tensor")
    slope_part = jnp.concatenate(
        [
            lax.dot_general(q_flat, bq_matrix, contract_last, preferred_element_type=jnp.float32),
            lax.dot_general(v_flat, bv_matrix, contract_last, preferred_element_type=jnp.float32),
        ],
        axis=1,
    )
    slopes = lax.psum(slope_part, "tensor")
    hidden_bf = hidden.astype(jnp.bfloat16)
    up_query = jnp.dot(
        hidden_bf[:, :rank_width], bq_matrix, preferred_element_type=jnp.float32
    ).astype(jnp.bfloat16)
    up_value = jnp.dot(
        hidden_bf[:, rank_width:], bv_matrix, preferred_element_type=jnp.float32
    ).astype(jnp.bfloat16)
    row_grad = jnp.sum(slopes * hidden_bf.astype(jnp.float32), axis=1).astype(jnp.bfloat16)
    weight_col = w_recv.reshape(-1, 1).astype(jnp.float32)
    grad_hidden = (weight_col * slopes).astype(jnp.bfloat16)
    grad_down = lax.dot_general(
        x_flat, grad_hidden, contract_first, preferred_element_type=jnp.float32
    ).astype(jnp.bfloat16)
    weighted = (weight_col * hidden).astype(jnp.bfloat16)
    grad_upq = lax.dot_general(
        weighted[:, :rank_width], q_flat, contract_first, preferred_element_type=jnp.float32
    ).astype(jnp.bfloat16)
    grad_upv = lax.dot_general(
        weighted[:, rank_width:], v_flat, contract_first, preferred_element_type=jnp.float32
    ).astype(jnp.bfloat16)
    back_query, back_value, back_grad = (
        lax.all_to_all(
            up_query.reshape(slot_count, row_count, feat_width),
            "expert",
            split_axis=0,
            concat_axis=0,
            tiled=True,
        ),
        lax.all_to_all(
            up_value.reshape(slot_count, row_count, value_width),
            "expert",
            split_axis=0,
            concat_axis=0,
            tiled=True,
        ),
        lax.all_to_all(
            row_grad.reshape(slot_count, row_count),
            "expert",
            split_axis=0,
            concat_axis=0,
            tiled=True,
        ),
    )
    scale_col = weights.reshape(-1, 1).astype(jnp.float32)
    out_query = (
        jnp.zeros((tok_count, feat_width), jnp.float32)
        .at[flat_idx]
        .add(scale_col * back_query.reshape(-1, feat_width).astype(jnp.float32))
    )
    out_value = (
        jnp.zeros((tok_count, value_width), jnp.float32)
        .at[flat_idx]
        .add(scale_col * back_value.reshape(-1, value_width).astype(jnp.float32))
    )
    slot_grad = jnp.sum(back_grad.astype(jnp.float32), axis=1)
    grad_mix = (
        jnp.zeros((slot_count,), jnp.float32).at[slot_order].set(slot_grad).reshape(1, requests, 4)
    )
    return (
        out_query.astype(jnp.bfloat16),
        out_value.astype(jnp.bfloat16),
        grad_down[None],
        grad_upq[None],
        grad_upv[None],
        grad_mix,
    )


LINE, PAIR = 4, 2
F32, BF16 = jnp.float32, jnp.bfloat16
MID = [(2, 4), (3, 5), (4, 2), (5, 3)]
OUT = [(2, 0), (3, 1), (4, 6), (5, 7)]
ROWS, COLS, SAME = ((0,), (0,)), ((1,), (1,)), ((1,), (0,))
LANES = 128
PREP_VMEM = 24


def cost(us):
    return pl.CostEstimate(flops=0, bytes_accessed=int(us * 3.0e6), transcendentals=0)


def to_place(array, place):
    return lax.ppermute(array, "expert", [(i, i ^ place) for i in range(LINE * PAIR)])


def other_core(part):
    return lax.ppermute(part, "tensor", [(0, 1), (1, 0)])


def line_gather(own):
    near = to_place(own, 2)
    inner = lax.ppermute(own, "expert", MID)
    second_out = lax.ppermute(inner, "expert", OUT)
    second_mid = lax.ppermute(near, "expert", MID)
    third_out = lax.ppermute(second_mid, "expert", OUT)
    return near, second_out, second_mid, inner, third_out


def dot(a, b, over):
    return lax.dot_general(a, b, (over, ((), ())), preferred_element_type=F32)


def call(kernel, outs, *ins, vmem=24, us=0):
    shapes = [jax.ShapeDtypeStruct(shape, dtype) for shape, dtype in outs]
    return pl.pallas_call(
        kernel,
        out_shape=shapes,
        in_specs=[pl.BlockSpec(memory_space=pltpu.VMEM)] * len(ins),
        out_specs=[pl.BlockSpec(memory_space=pltpu.VMEM)] * len(outs),
        compiler_params=pltpu.CompilerParams(vmem_limit_bytes=vmem * 1024 * 1024),
        cost_estimate=cost(us),
    )(*ins)


def members(request_row, requests):
    tok = request_row.shape[1]
    ids = lax.broadcasted_iota(jnp.int32, (requests, tok), 0)
    return ids == jnp.broadcast_to(request_row, (requests, tok))


def picked(me_ref, ra_ref, rc_ref, k, place):
    found = (jnp.broadcast_to(ra_ref[0, k : k + 1, :], place.shape) ^ me_ref[0]) == place
    return found & jnp.broadcast_to(rc_ref[...] > k, place.shape)


def prepare(me_ref, small, bq, bv, gq, gv, x, a, b_ref, gw_ref, x_ref, a_ref, small_ref, tr_ref, ra_ref, rc_ref, rm_ref, sems):
    wide = x.shape[1]
    rank, narrow = bv.shape[1:]
    full = wide + narrow
    step = rank * narrow // wide
    pairs = [
        (small, small_ref),
        (bq.at[0], b_ref.at[pl.ds(0, rank)]),
        (gq, gw_ref.at[:, pl.ds(0, wide)]),
        (gv, gw_ref.at[:, pl.ds(wide, narrow)]),
        (x, x_ref),
        (a, a_ref),
    ]
    for i in range(rank // step):
        dst = b_ref.at[pl.ds(rank, step), pl.ds(i * narrow, narrow)]
        pairs.append((bv.at[0, pl.ds(i * step, step)], dst))
    copies = [pltpu.make_async_copy(src, dst, sems.at[i]) for i, (src, dst) in enumerate(pairs)]
    for copy in copies:
        copy.start()
    copies[0].wait()
    held = rc_ref.shape[1]
    tr_ref[...] = small_ref[0:1, :].astype(jnp.int32)
    ra_ref[0] = small_ref[8:12, :held].astype(jnp.int32)
    rc_ref[...] = small_ref[16:17, :held].astype(jnp.int32)
    rm_ref[0] = small_ref[24:28, :held].astype(BF16)
    requests = ra_ref.shape[2]
    place = lax.broadcasted_iota(jnp.int32, (LANES, requests), 0)
    total = jnp.zeros((LANES, requests), F32)
    for k in range(4):
        mix = jnp.broadcast_to(rm_ref[0, k : k + 1, :].astype(F32), place.shape)
        total = total + jnp.where(picked(me_ref, ra_ref, rc_ref, k, place), mix, 0.0)
    high = total.astype(BF16)
    low = (total - high.astype(F32)).astype(BF16)
    member = jnp.where(members(tr_ref[...], requests), 1.0, 0.0).astype(BF16)
    gw_ref[:, full : full + LANES] = dot(member, high, ((0,), (1,))).astype(BF16)
    gw_ref[:, full + LANES :] = dot(member, low, ((0,), (1,))).astype(BF16)
    for copy in copies[1:]:
        copy.wait()


def weight_of(gw_ref, place):
    full = gw_ref.shape[1] - 2 * LANES
    high = gw_ref[:, full : full + LANES][:, place : place + 1].astype(F32)
    low = gw_ref[:, full + LANES :][:, place : place + 1].astype(F32)
    return high + low


def b_parts(b, narrow):
    rows, wide = b.shape
    blocks = wide // narrow
    step = rows // (blocks + 1)
    last = b[blocks * step :, :]
    value = jnp.concatenate([last[:, i * narrow : (i + 1) * narrow] for i in range(blocks)], axis=0)
    return b[: blocks * step, :], value


def hidden_of(x, rows, a_ref, ax_ref, out_ref):
    rank2 = a_ref.shape[1]
    out_ref[rows, :rank2] = dot(x, a_ref[...], SAME).astype(out_ref.dtype)
    out_ref[rows, rank2 : 2 * rank2] = dot(x, ax_ref[...], SAME).astype(out_ref.dtype)


def slopes_of(b, rows, first, gw_ref, gx_ref, out_ref):
    full = gw_ref.shape[1] - 2 * LANES
    wide = b.shape[1]
    bq, bv = b_parts(b, full - wide)
    rank2 = 2 * bq.shape[0]
    for i, g_ref in enumerate((gw_ref, gx_ref)):
        part_q = dot(g_ref[:, :wide], bq, COLS)
        part_v = dot(g_ref[:, wide:full], bv, COLS)
        out_ref[rows, first + i * rank2 : first + (i + 1) * rank2] = jnp.concatenate([part_q, part_v], axis=1).astype(out_ref.dtype)


def products_early(x0, x1, xo, xm, b0, b1, bo, bm, a_ref, ax_ref, gw_ref, gx_ref, h_ref, s_ref, x2_ref, b2_ref):
    count = x2_ref.shape[0]
    x2_ref[...] = xo[...] + xm[...]
    b2_ref[...] = bo[...] + bm[...]
    for j, (x, b) in enumerate(((x0, b0), (x1, b1), (x2_ref, b2_ref))):
        rows = slice(j * count, (j + 1) * count)
        hidden_of(x[...], rows, a_ref, ax_ref, h_ref)
        slopes_of(b[...], rows, 0, gw_ref, gx_ref, s_ref)


def products_late(xi, xo, bi, bo, a_ref, ax_ref, gw_ref, gx_ref, out_ref, x3_ref, b3_ref):
    x3_ref[...] = xi[...] + xo[...]
    b3_ref[...] = bi[...] + bo[...]
    rows = slice(0, x3_ref.shape[0])
    hidden_of(x3_ref[...], rows, a_ref, ax_ref, out_ref)
    slopes_of(b3_ref[...], rows, 2 * a_ref.shape[1], gw_ref, gx_ref, out_ref)


def split_early(m_ref, mr_ref, s_ref, sr_ref, gw_ref, gx_ref, sl_ref, near_ref, *far_refs):
    count = gw_ref.shape[0]
    both = m_ref.shape[1]
    for j in range(LINE - 1):
        rows = slice(j * count, (j + 1) * count)
        cols = pl.ds(j * both, both)
        slope = s_ref[rows, :].astype(F32) + sr_ref[rows, :].astype(F32)
        sl_ref[rows, :] = slope
        blocks = near_ref.at[:, cols], far_refs[j]
        fill_blocks(j, m_ref[rows, :].astype(F32) + mr_ref[rows, :].astype(F32), slope, gw_ref, gx_ref, *blocks)


def pack_slots(near_ref, f0, f1, f2, *out_refs):
    rank2 = out_refs[0].shape[1] // 4
    for j, (far_ref, out_ref) in enumerate(zip((f0, f1, f2), out_refs)):
        for half in range(2):
            first = (2 * j + half) * rank2
            out_ref[:, 2 * half * rank2 : (2 * half + 1) * rank2] = near_ref[:, first : first + rank2]
            out_ref[:, (2 * half + 1) * rank2 : (2 * half + 2) * rank2] = far_ref[:, half * rank2 : (half + 1) * rank2]


def split_late(m_ref, r_ref, gw_ref, gx_ref, sl_ref, near_ref, far_ref):
    total = m_ref[...].astype(F32) + r_ref[...].astype(F32)
    half = total.shape[1] // 2
    sl_ref[...] = total[:, half:]
    fill_blocks(LINE - 1, total[:, :half], total[:, half:], gw_ref, gx_ref, near_ref, far_ref)


def fill_blocks(j, hidden, slope, gw_ref, gx_ref, near_ref, far_ref):
    rank2 = near_ref.shape[1] // 2
    hidden = hidden.astype(BF16)
    near_ref[:, :rank2] = hidden[:, :rank2]
    far_ref[:, :rank2] = hidden[:, rank2:]
    near_ref[:, rank2:] = (weight_of(gw_ref, 2 * j) * slope[:, :rank2]).astype(BF16)
    far_ref[:, rank2:] = (weight_of(gx_ref, 2 * j + 1) * slope[:, rank2:]).astype(BF16)


def grad_b_parts(wide, wt_ref, gw_ref, gx_ref, *p_refs):
    count = gw_ref.shape[0]
    rank, full = p_refs[0].shape
    slots = len(p_refs)
    left = [(2 * j + i) * rank for i in range(2) for j in range(slots)]
    both = wt_ref[...]
    both = jnp.concatenate([both[:, c : c + rank] for c in left], axis=1)
    own, other = both[:count], both[count:]
    half = slots * rank
    part_q = dot(own[:, :half], gw_ref[:, :wide], ROWS) + dot(other[:, :half], gx_ref[:, :wide], ROWS)
    part_v = dot(own[:, half:], gw_ref[:, wide:full], ROWS) + dot(other[:, half:], gx_ref[:, wide:full], ROWS)
    for j, p_ref in enumerate(p_refs):
        p_ref[:, :wide] = part_q[j * rank : (j + 1) * rank].astype(p_ref.dtype)
        p_ref[:, wide:] = part_v[j * rank : (j + 1) * rank].astype(p_ref.dtype)


def grad_b_sum(p0, p1, p2, p3, q_ref, v_ref):
    wide = q_ref.shape[2]
    total = p0[...] + p1[...].astype(F32) + p2[...].astype(F32) + p3[...].astype(F32)
    q_ref[0] = total[:, :wide].astype(BF16)
    v_ref[0] = total[:, wide:].astype(BF16)


def outputs_part(
    c0, c1, c2, n3, f3, gw_ref, gx_ref, b0, b1, b2, b3, s_ref, s3_ref, own_ref, sent_ref, rg_ref, wt_ref
):
    count, full = own_ref.shape
    wide = b0.shape[1]
    parts = [b_parts(b[...], full - wide) for b in (b0, b1, b2, b3)]
    bq = jnp.concatenate([part[0] for part in parts], axis=0)
    bv = jnp.concatenate([part[1] for part in parts], axis=0)
    rank = bq.shape[0] // LINE
    rank2 = 2 * rank
    owns = [c[:, :rank2] for c in (c0, c1, c2, n3)]
    others = [c[:, rank2 : 2 * rank2] for c in (c0, c1, c2)] + [f3[:, :rank2]]
    for j in range(LINE):
        cols = slice(j * rank2, (j + 1) * rank2)
        own = weight_of(gw_ref, 2 * j) * owns[j].astype(F32)
        other = weight_of(gx_ref, 2 * j + 1) * others[j].astype(F32)
        wt_ref[:count, cols] = own.astype(BF16)
        wt_ref[count:, cols] = other.astype(BF16)
    both = wt_ref[...]
    q = jnp.concatenate([both[:, j * rank2 : j * rank2 + rank] for j in range(LINE)], axis=1)
    v = jnp.concatenate([both[:, j * rank2 + rank : (j + 1) * rank2] for j in range(LINE)], axis=1)
    out_q = dot(q, bq, SAME)
    out_v = dot(v, bv, SAME)
    own_ref[:, :wide] = out_q[:count]
    own_ref[:, wide:] = out_v[:count]
    sent_ref[:, :wide] = out_q[count:].astype(BF16)
    sent_ref[:, wide:full] = out_v[count:].astype(BF16)
    lane = lax.broadcasted_iota(jnp.int32, (count, LANES), 1)
    for i, blocks in enumerate((owns, others)):
        cols = slice(i * rank2, (i + 1) * rank2)
        found = jnp.zeros((count, LANES), F32)
        for j, block in enumerate(blocks):
            slope = s_ref[j * count : (j + 1) * count, cols] if j < 3 else s3_ref[:, cols]
            grad = jnp.sum(slope * block.astype(F32), axis=1, keepdims=True)
            found = jnp.where(lane == 2 * j + i, jnp.broadcast_to(grad, found.shape), found)
        if i == 0:
            rg_ref[...] = found.astype(BF16)
        else:
            sent_ref[:, full:] = found.astype(BF16)


def outputs_sum(me_ref, own_ref, sent_ref, rg_ref, tr_ref, ra_ref, rc_ref, q_ref, v_ref, mix_ref):
    full = own_ref.shape[1]
    wide = q_ref.shape[1]
    total = own_ref[...] + sent_ref[:, :full].astype(F32)
    q_ref[...] = total[:, :wide].astype(BF16)
    v_ref[...] = total[:, wide:].astype(BF16)
    requests = ra_ref.shape[2]
    row_grad = rg_ref[...] + sent_ref[:, full:]
    member = jnp.where(members(tr_ref[...], requests), 1.0, 0.0).astype(BF16)
    req_grad = dot(row_grad, member, ((0,), (1,)))
    place = lax.broadcasted_iota(jnp.int32, (LANES, requests), 0)
    for k in range(4):
        found = jnp.where(picked(me_ref, ra_ref, rc_ref, k, place), req_grad, 0.0)
        mix_ref[0, k : k + 1, :] = jnp.sum(found, axis=0, keepdims=True)


def pair_plan(
    tokens,
    grad_query,
    grad_value,
    a_proj,
    b_query,
    b_value,
    token_request,
    req_adapter,
    req_count,
    req_mix,
):
    rank = b_query.shape[1]
    rank2 = 2 * rank
    wide = grad_query.shape[1]
    full = wide + grad_value.shape[1]
    count = tokens.shape[0]
    me = lax.axis_index("expert").astype(jnp.int32).reshape(1)
    block = ((count, rank2), BF16)
    b_block = ((rank, full), BF16)
    x_block = (tokens.shape, BF16)
    adapters = jnp.swapaxes(req_adapter, 1, 2)
    mixes = jnp.swapaxes(req_mix, 1, 2)
    rows = (token_request, adapters[0], req_count, mixes[0])
    rows = [jnp.pad(r.astype(F32), ((0, 8 - r.shape[0]), (0, count - r.shape[1]))) for r in rows]
    small = jnp.concatenate(rows, axis=0)
    pair = ((count, 2 * rank2), BF16)
    early = ((count, 3 * rank2), BF16)

    x1, xi = to_place(tokens, 2), lax.ppermute(tokens, "expert", MID)
    a_other = to_place(a_proj[0], 1)
    b0, gw, x0, a_own = call_prepare(
        me, small, (token_request, adapters, req_count, mixes),
        b_query, b_value, grad_query, grad_value, tokens, a_proj[0],
    )
    b1, bi = to_place(b0, 2), lax.ppermute(b0, "expert", MID)
    x1, a_other = lax.optimization_barrier((x1, a_other))
    xm = lax.ppermute(x1, "expert", MID)
    xo = lax.ppermute(xi, "expert", OUT)
    bo, bm = lax.ppermute(bi, "expert", OUT), lax.ppermute(b1, "expert", MID)
    gx = to_place(gw, 1)
    xo3 = lax.ppermute(xm, "expert", OUT)
    bo3 = lax.ppermute(bm, "expert", OUT)

    wide_block = (b0.shape, BF16)
    m, ms, x2, b2 = call(
        products_early,
        [((3 * count, 2 * rank2), BF16), ((3 * count, 2 * rank2), BF16), x_block, wide_block],
        x0, x1, xo, xm, b0, b1, bo, bm, a_own, a_other, gw, gx,
    )
    sl, near, *far = call(
        split_early,
        [((3 * count, 2 * rank2), F32), ((count, 6 * rank2), BF16)] + [pair] * 3,
        m, other_core(m), ms, other_core(ms), gw, gx,
    )
    (xo3,) = after(sl, xo3)
    far = [to_place(part, 1) for part in far]
    near, bo3 = lax.optimization_barrier((near, bo3))
    c0, c1, c2 = call(pack_slots, [((count, 4 * rank2), BF16)] * 3, near, *far)
    c1, c2 = to_place(c1, 2), to_place(c2, 4)
    h3, x3, b3 = call(
        products_late,
        [((count, 4 * rank2), BF16), x_block, wide_block],
        xi, xo3, bi, bo3, a_own, a_other, gw, gx,
    )
    rh = other_core(h3)
    c1, c2 = after(h3, c1, c2)
    grad_a = dot(x0, c0[:, 2 * rank2 :], ROWS) + dot(x1, c1[:, 2 * rank2 :], ROWS)
    rh, grad_a = lax.optimization_barrier((rh, grad_a))
    sl3, n3, f3 = call(
        split_late,
        [((count, 2 * rank2), F32), pair, pair],
        h3, rh, gw, gx,
    )
    n3, f3 = to_place(n3, 6), to_place(f3, 7)
    (c2,) = after(sl3, c2)
    grad_a = grad_a + dot(x2, c2[:, 2 * rank2 :], ROWS)
    n3, f3, grad_a = lax.optimization_barrier((n3, f3, grad_a))
    out_own, sent, rg, wt = call(
        outputs_part,
        [((count, full), F32), ((count, full + LANES), BF16), ((count, LANES), BF16), ((2 * count, LINE * rank2), BF16)],
        c0, c1, c2, n3, f3, gw, gx, b0, b1, b2, b3, sl, sl3,
    )
    sent = to_place(sent, 1)
    p0, p1, p2, p3 = call(
        functools.partial(grad_b_parts, wide), [((rank, full), F32)] + [b_block] * 3, wt, gw, gx
    )
    p1, p2, p3 = to_place(p1, 2), to_place(p2, 4), to_place(p3, 6)
    (f3s,) = after(p0, f3)
    grad_a_other = (grad_a[:, rank2:] + dot(x3, f3s[:, rank2:], ROWS)).astype(BF16)
    (n3s,) = after(grad_a_other, n3)
    grad_a = grad_a[:, :rank2] + dot(x3, n3s[:, rank2:], ROWS)
    (sent,) = after(grad_a, sent)
    out_query, out_value, grad_mix = call_sum(
        me, out_own, sent, rg, token_request, adapters, req_count, grad_query, grad_value
    )
    (grad_a,) = after(out_query, grad_a)
    grad_a = grad_a + to_place(grad_a_other, 1).astype(F32)
    (p1,) = after(grad_a, p1)
    grad_bq, grad_bv = call(grad_b_sum, [(b_query.shape, BF16), (b_value.shape, BF16)], p0, p1, p2, p3)
    return out_query, out_value, grad_a.astype(BF16)[None], grad_bq, grad_bv, jnp.swapaxes(grad_mix, 1, 2)


def after(earlier, *arrays):
    return lax.optimization_barrier((*arrays, earlier))[:-1]


def call_with_me(kernel, outs, *ins, us=0):
    shapes = [jax.ShapeDtypeStruct(shape, dtype) for shape, dtype in outs]
    return pl.pallas_call(
        kernel,
        out_shape=shapes,
        in_specs=[pl.BlockSpec(memory_space=pltpu.SMEM)] + [pl.BlockSpec(memory_space=pltpu.VMEM)] * (len(ins) - 1),
        out_specs=[pl.BlockSpec(memory_space=pltpu.VMEM)] * len(outs),
        compiler_params=pltpu.CompilerParams(vmem_limit_bytes=24 * 1024 * 1024),
        cost_estimate=cost(us),
    )(*ins)


def call_prepare(me, *args):
    small, (request, adapters, counts, mix), b_query, b_value, grad_query, grad_value, x, a = args
    ins = (small, *args[2:])
    rank, wide = b_query.shape[1:]
    narrow = b_value.shape[2]
    step = rank * narrow // wide
    outs = [
        (rank + step, wide),
        (grad_query.shape[0], wide + narrow + 2 * LANES),
        x.shape,
        a.shape,
    ]
    return pl.pallas_call(
        prepare,
        out_shape=[jax.ShapeDtypeStruct(shape, BF16) for shape in outs],
        in_specs=[pl.BlockSpec(memory_space=pltpu.SMEM)] + [pl.BlockSpec(memory_space=pltpu.HBM)] * len(ins),
        out_specs=[pl.BlockSpec(memory_space=pltpu.VMEM)] * len(outs),
        scratch_shapes=[pltpu.VMEM(i.shape, i.dtype) for i in (small, request, adapters, counts, mix)]
        + [pltpu.SemaphoreType.DMA((len(ins) - 1 + rank // step,))],
        compiler_params=pltpu.CompilerParams(vmem_limit_bytes=PREP_VMEM * 1024 * 1024),
        cost_estimate=cost(0),
    )(me, *ins)


def call_sum(me, own, sent, rg, token_request, adapters, req_count, grad_query, grad_value):
    outs = [(grad_query.shape, BF16), (grad_value.shape, BF16), (adapters.shape, F32)]
    return call_with_me(outputs_sum, outs, me, own, sent, rg, token_request, adapters, req_count, us=0)


def solution(mesh):
    in_specs = (
        P(("groups", "expert"), "tensor"),
        P(("groups", "expert"), "tensor"),
        P(("groups", "expert"), "tensor"),
        P(("groups", "expert"), "tensor", None),
        P(("groups", "expert"), None, "tensor"),
        P(("groups", "expert"), None, "tensor"),
        P(("groups", "expert"), None),
        P(("groups", "expert"), None, None),
        P(("groups", "expert"), None),
        P(("groups", "expert"), None, None),
    )
    out_specs = (
        P(("groups", "expert"), "tensor"),
        P(("groups", "expert"), "tensor"),
        P(("groups", "expert"), "tensor", None),
        P(("groups", "expert"), None, "tensor"),
        P(("groups", "expert"), None, "tensor"),
        P(("groups", "expert"), None, None),
    )
    shards = pair_plan if mesh.shape["expert"] == LINE * PAIR else row_exchange
    return jax.shard_map(shards, mesh=mesh, in_specs=in_specs, out_specs=out_specs, check_vma=False)
```
